128 devices in a mesh: group: 8 (over y, x_hi), member: 16 (over z, x_lo, core).
Axes of the slice: x: 4 (x_hi: 2, x_lo: 2; x = x_hi * 2 + x_lo), y: 4, z: 4, core: 2. Of those that a mesh axis runs over, the one named last changes fastest.
Arguments:
- embeddings: float32 [131072, 256], P(('group', 'member')), may hold values from -24 to 24, as said below
- operators: float32 [16, 256, 256], replicated, as said below
- plan: int32 [4], replicated, may hold values from 1 to 127, as said below
- relations: int32 [4, 1024], P(None, ('group', 'member')), may hold values from 0 to 15
Outputs:
- new_embeddings: float32 [131072, 256], P(('group', 'member'))
- new_operators: float32 [16, 256, 256], replicated
The draws below stay inside these ranges and needn't reach their ends.
Inputs may be any that keep to these rules, and one draw needn't show every extreme that they name: The 4 values are distinct, so every round pairs distinct partitions two by two; both 1 and 127 occur in every plan. `embeddings`: rows are of order one; some rows may be several times larger. `operators`: each operator is the identity plus a dense full-rank part.
All inputs are finite; a program needn't handle non-finite values.
Results may differ from the reference program's by a relative error of at most 0.015.
The reference program's roundings to bfloat16 on the way count: a program that leaves them out, or rounds other values in their place, can miss the bound.
Values may be sent and summed in bfloat16 or wider, within the bound.
No kernel may reach another device: no remote copies, remote signals or barrier semaphores. Data moves between devices by JAX's collectives and lax.ppermute only.
A program may use at most 128 MiB of HBM per device.

```python
import math
import jax
import jax.numpy as jnp
from jax import lax

EMBED_WIDTH = 256
RELS = 16
ROWS = 1024
RB = 128
NEG = 1024
ROUNDS = 4
NODES = 131072
BLOCKS = 1024
DEVICES = 128


def draw_embeddings(key, part):
    normal_part = jax.random.normal(jax.random.fold_in(key, 11), (NODES, EMBED_WIDTH), jnp.float32)
    return jnp.clip(normal_part, -6.0, 6.0)


def draw_operators(key, part):
    noise = jax.random.normal(jax.random.fold_in(key, 21), (RELS, EMBED_WIDTH, EMBED_WIDTH), jnp.float32)
    return jnp.eye(EMBED_WIDTH, dtype=jnp.float32)[None, :, :] + 0.6 / jnp.sqrt(jnp.float32(EMBED_WIDTH)) * noise


def draw_plan(key, part):
    middle = jax.random.permutation(jax.random.fold_in(key, 31), DEVICES - 3) + 2
    ends = jnp.array([1, DEVICES - 1], dtype=jnp.int32)
    values = jnp.concatenate([ends, middle[:ROUNDS - 2].astype(jnp.int32)])
    shuffled = jax.random.permutation(jax.random.fold_in(key, 32), values)
    return shuffled.astype(jnp.int32)


def set_ends(entries, key, smallest, largest):
    index_at = [jax.random.randint(jax.random.fold_in(key, axis), (), 0, length) for axis, length in enumerate(entries.shape)]
    widest = entries.shape.index(max(entries.shape))
    neighbour = index_at[:widest] + [(index_at[widest] + 1) % entries.shape[widest]] + index_at[widest + 1:]
    return entries.at[tuple(index_at)].set(smallest).at[tuple(neighbour)].set(largest)


def setup_inputs(seed: int = 0) -> dict:
    streams_of = jax.random.split(jax.random.key(seed), 5)
    return {
        "embeddings": draw_embeddings(jax.random.fold_in(streams_of[4], 71), 0),
        "operators": draw_operators(jax.random.fold_in(streams_of[4], 71), 0),
        "plan": draw_plan(jax.random.fold_in(streams_of[4], 71), 0),
        "relations": set_ends(jax.random.randint(streams_of[3], (ROUNDS, BLOCKS), 0, RELS), jax.random.fold_in(streams_of[3], 1), 0, RELS - 1).astype(jnp.int32),
    }


embed_rate = 1.0
operator_rate = 0.02

def bucket_grads(own_rows, partner, rel_ids, ops_table):
    count_of_rows = own_rows.shape[0]
    block_tiles = rel_ids.shape[0]
    block_rows = count_of_rows // block_tiles
    neg_blocks = count_of_rows // NEG
    scale_of_scores = 1.0 / math.sqrt(EMBED_WIDTH)
    onehot = (rel_ids[:, None] == jnp.arange(RELS, dtype=jnp.int32)[None, :]).astype(jnp.float32)
    picked_rows = jnp.dot(onehot, ops_table, precision=lax.Precision.HIGHEST).astype(jnp.bfloat16).reshape(block_tiles, EMBED_WIDTH, EMBED_WIDTH)
    picked_rows_wide = picked_rows.astype(jnp.float32)
    local_block_tiles = own_rows.reshape(block_tiles, block_rows, EMBED_WIDTH).astype(jnp.float32)
    query_rows = jnp.einsum('rux,rxp->rup', local_block_tiles, picked_rows_wide).astype(jnp.bfloat16)
    query_groupings = query_rows.reshape(neg_blocks, NEG, EMBED_WIDTH).astype(jnp.float32)
    partner_groupings = partner.reshape(neg_blocks, NEG, EMBED_WIDTH).astype(jnp.float32)
    score_matrix = jnp.einsum('mfn,mon->mfo', query_groupings, partner_groupings) * scale_of_scores
    row_prob = jax.nn.softmax(score_matrix, axis=2)
    col_prob = jax.nn.softmax(score_matrix, axis=1)
    identity = jnp.eye(NEG, dtype=jnp.float32)
    score_gradient = ((row_prob - identity + (col_prob - identity)) * scale_of_scores).astype(jnp.bfloat16).astype(jnp.float32)
    query_gradient = jnp.einsum('rti,rie->rte', score_gradient, partner_groupings).astype(jnp.bfloat16)
    right_gradient = jnp.einsum('lfv,lfh->lvh', score_gradient, query_groupings).astype(jnp.bfloat16).reshape(count_of_rows, EMBED_WIDTH)
    query_gradient_blocks = query_gradient.reshape(block_tiles, block_rows, EMBED_WIDTH).astype(jnp.float32)
    left_gradient = jnp.einsum('jts,jus->jtu', query_gradient_blocks, picked_rows_wide).reshape(count_of_rows, EMBED_WIDTH)
    block_gradient = jnp.einsum('vmi,vmg->vig', local_block_tiles, query_gradient_blocks).reshape(block_tiles, EMBED_WIDTH * EMBED_WIDTH)
    op_grad = jnp.dot(onehot.T, block_gradient, precision=lax.Precision.HIGHEST)
    return (left_gradient, right_gradient, op_grad)

def reference(embeddings, operators, plan, relations):
    ops_bf = operators.astype(jnp.bfloat16)
    ops_table = lax.optimization_barrier(ops_bf).astype(jnp.float32).reshape(RELS, EMBED_WIDTH * EMBED_WIDTH)
    embeds = embeddings.reshape(DEVICES, ROWS, EMBED_WIDTH)
    total = jnp.zeros((RELS, EMBED_WIDTH * EMBED_WIDTH), jnp.float32)
    index_list = jnp.arange(DEVICES, dtype=jnp.int32)
    for round_index in range(ROUNDS):
        partner_index = jnp.bitwise_xor(index_list, plan[round_index]).astype(jnp.int32)
        left_rows = embeds.astype(jnp.bfloat16)
        right_rows = left_rows[partner_index]
        rel_rows = relations[round_index].reshape(DEVICES, ROWS // RB)

        def step_one(carry, items):
            left_gradient, right_gradient, op_grad = bucket_grads(items[0], items[1], items[2], ops_table)
            return (carry + op_grad, (left_gradient, right_gradient))
        total, outputs = lax.scan(step_one, total, (left_rows, right_rows, rel_rows))
        left_gradient, right_gradient = outputs
        returned = right_gradient[partner_index].astype(jnp.float32)
        embeds = embeds - embed_rate * (left_gradient + returned)
    new_operators = operators - operator_rate * total.reshape(RELS, EMBED_WIDTH, EMBED_WIDTH)
    return (embeds.reshape(NODES, EMBED_WIDTH), new_operators)
```

```python
import functools
import math

import jax
import jax.numpy as jnp
from jax import lax
from jax.experimental import pallas as pl
from jax.experimental.pallas import tpu as pltpu
from jax.sharding import PartitionSpec as P

ROUNDS = 4
AXES = ("group", "member")
CHUNK = 256
F32 = jnp.float32
BF16 = jnp.bfloat16

embed_rate = 1.0
operator_rate = 0.02


def dot_nt(a, b):
    return lax.dot_general(a, b, (((1,), (1,)), ((), ())), preferred_element_type=F32)


def dot_nn(a, b):
    return lax.dot_general(a, b, (((1,), (0,)), ((), ())), preferred_element_type=F32)


def dot_tn(a, b):
    return lax.dot_general(a, b, (((0,), (0,)), ((), ())), preferred_element_type=F32)


def two_way_gradient(x_ref, y_ref, s_ref, emit):
    rows, width = x_ref.shape
    chunks = rows // CHUNK
    scale = 1.0 / math.sqrt(width)
    in_bits = scale * math.log2(math.e)
    shift = -math.log2(scale)
    row_norm = []
    col_max = col_sum = None
    for i in range(chunks):
        block = pl.ds(i * CHUNK, CHUNK)
        s = dot_nt(x_ref[block, :], y_ref[...]) * in_bits
        s_ref[block, :] = s
        row_max = jnp.max(s, axis=1, keepdims=True)
        row_sum = jnp.sum(jnp.exp2(s - row_max), axis=1, keepdims=True)
        row_norm.append(row_max + (jnp.log2(row_sum) + shift))
        here_max = jnp.max(s, axis=0, keepdims=True)
        if i == 0:
            col_max = here_max
            col_sum = jnp.sum(jnp.exp2(s - col_max), axis=0, keepdims=True)
        else:
            new_max = jnp.maximum(col_max, here_max)
            col_sum = col_sum * jnp.exp2(col_max - new_max) + jnp.sum(
                jnp.exp2(s - new_max), axis=0, keepdims=True
            )
            col_max = new_max
    col_norm = col_max + (jnp.log2(col_sum) + shift)
    for i in range(chunks):
        block = pl.ds(i * CHUNK, CHUNK)
        s = s_ref[block, :]
        d = jnp.exp2(s - row_norm[i]) + jnp.exp2(s - col_norm)
        at = lax.broadcasted_iota(jnp.int32, d.shape, 0) + i * CHUNK
        d = jnp.where(at == lax.broadcasted_iota(jnp.int32, d.shape, 1), d - 2.0 * scale, d)
        emit(i, dot_nn(d.astype(BF16), y_ref[...]))


def round_kernel(
    rel_ref, rel_far_ref, e_ref, l_ref, r_ref, ops_ref, g_in_ref,
    e_out_ref, l_out_ref, g_ref, q_ref, q_far_ref, dq_ref, s_ref,
):
    rows = e_ref.shape[0]
    blocks = rel_ref.shape[0]
    size = rows // blocks
    for b in range(blocks):
        block = pl.ds(b * size, size)
        q_ref[block, :] = dot_nn(l_ref[block, :], ops_ref[rel_ref[b]]).astype(BF16)
        q_far_ref[block, :] = dot_nn(r_ref[block, :], ops_ref[rel_far_ref[b]]).astype(BF16)

    def own(i, value):
        dq_ref[pl.ds(i * CHUNK, CHUNK), :] = value.astype(BF16)

    two_way_gradient(q_ref, r_ref, s_ref, own)
    for b in range(blocks):
        block = pl.ds(b * size, size)
        e_out_ref[block, :] = dot_nt(dq_ref[block, :], ops_ref[rel_ref[b]])

    def far(i, value):
        block = pl.ds(i * CHUNK, CHUNK)
        moved = e_ref[block, :] - embed_rate * (e_out_ref[block, :] + value.astype(BF16).astype(F32))
        e_out_ref[block, :] = moved
        l_out_ref[block, :] = moved.astype(BF16)

    two_way_gradient(l_ref, q_far_ref, s_ref, far)
    g_ref[...] = g_in_ref[...]
    for b in range(blocks):
        block = pl.ds(b * size, size)
        g_ref[rel_ref[b]] += dot_tn(l_ref[block, :], dq_ref[block, :])


def run_round(rel, rel_far, e, left, right, ops, g):
    rows, width = e.shape
    vmem = pl.BlockSpec(memory_space=pltpu.VMEM)
    smem = pl.BlockSpec(memory_space=pltpu.SMEM)
    return pl.pallas_call(
        round_kernel,
        out_shape=(
            jax.ShapeDtypeStruct(e.shape, F32),
            jax.ShapeDtypeStruct(e.shape, BF16),
            jax.ShapeDtypeStruct(g.shape, F32),
        ),
        in_specs=[smem, smem] + [vmem] * 5,
        out_specs=(vmem,) * 3,
        input_output_aliases={6: 2},
        scratch_shapes=[
            pltpu.VMEM((rows, width), BF16),
            pltpu.VMEM((rows, width), BF16),
            pltpu.VMEM((rows, width), BF16),
            pltpu.VMEM((rows, rows), F32),
        ],
        compiler_params=pltpu.CompilerParams(vmem_limit_bytes=48 * 2**20),
    )(rel, rel_far, e, left, right, ops, g)


def fetch(left, rel, mask):
    count = lax.axis_size(AXES)

    def by(m):
        route = [(i, i ^ m) for i in range(count)]
        return lambda a, b: (lax.ppermute(a, AXES, route), lax.ppermute(b, AXES, route))

    return lax.switch(mask - 1, [by(m) for m in range(1, count)], left, rel)


def shards(embeddings, operators, plan, relations):
    ops = operators.astype(BF16)
    e = embeddings
    left = e.astype(BF16)
    g = jnp.zeros(operators.shape, F32)
    for r in range(ROUNDS):
        right, rel_far = fetch(left, relations[r], plan[r])
        e, left, g = run_round(relations[r], rel_far, e, left, right, ops, g)
    count = lax.axis_size(AXES)
    flat = g.astype(BF16).reshape(count, -1, operators.shape[2])
    parts = lax.all_to_all(flat, AXES, 0, 0, tiled=True)
    mine = jnp.sum(parts.astype(F32), axis=0, keepdims=True).astype(BF16)
    summed = lax.all_to_all(jnp.broadcast_to(mine, flat.shape), AXES, 0, 0, tiled=True)
    new_operators = operators - operator_rate * summed.astype(F32).reshape(operators.shape)
    return (e, new_operators)


def solution(mesh):
    return jax.shard_map(
        shards,
        mesh=mesh,
        in_specs=(P(AXES, None), P(), P(), P(None, AXES)),
        out_specs=(P(AXES, None), P()),
        check_vma=False,
    )
```

```python
import functools
import math

import jax
import jax.numpy as jnp
from jax import lax
from jax.experimental import pallas as pl
from jax.experimental.pallas import tpu as pltpu
from jax.sharding import PartitionSpec as P

ROUNDS = 4
AXES = ("chip", "core")
ID_ROWS = 16
CHUNK = 256
F32 = jnp.float32
BF16 = jnp.bfloat16

embed_rate = 1.0
operator_rate = 0.02


def dot_nt(a, b):
    return lax.dot_general(a, b, (((1,), (1,)), ((), ())), preferred_element_type=F32)


def dot_nn(a, b):
    return lax.dot_general(a, b, (((1,), (0,)), ((), ())), preferred_element_type=F32)


def dot_tn(a, b):
    return lax.dot_general(a, b, (((0,), (0,)), ((), ())), preferred_element_type=F32)


def two_way_gradient(x_ref, y_ref, s_ref, rows, emit):
    width = x_ref.shape[1]
    every = pl.ds(0, rows)
    chunks = rows // CHUNK
    scale = 1.0 / math.sqrt(width)
    in_bits = scale * math.log2(math.e)
    shift = -math.log2(scale)
    row_norm = []
    col_max = col_sum = None
    for i in range(chunks):
        block = pl.ds(i * CHUNK, CHUNK)
        s = dot_nt(x_ref[block, :], y_ref[every, :]) * in_bits
        s_ref[block, :] = s
        row_max = jnp.max(s, axis=1, keepdims=True)
        row_sum = jnp.sum(jnp.exp2(s - row_max), axis=1, keepdims=True)
        row_norm.append(row_max + (jnp.log2(row_sum) + shift))
        here_max = jnp.max(s, axis=0, keepdims=True)
        if i == 0:
            col_max = here_max
            col_sum = jnp.sum(jnp.exp2(s - col_max), axis=0, keepdims=True)
        else:
            new_max = jnp.maximum(col_max, here_max)
            col_sum = col_sum * jnp.exp2(col_max - new_max) + jnp.sum(
                jnp.exp2(s - new_max), axis=0, keepdims=True
            )
            col_max = new_max
    col_norm = col_max + (jnp.log2(col_sum) + shift)
    for i in range(chunks):
        block = pl.ds(i * CHUNK, CHUNK)
        s = s_ref[block, :]
        d = jnp.exp2(s - row_norm[i]) + jnp.exp2(s - col_norm)
        at = lax.broadcasted_iota(jnp.int32, d.shape, 0) + i * CHUNK
        d = jnp.where(at == lax.broadcasted_iota(jnp.int32, d.shape, 1), d - 2.0 * scale, d)
        emit(i, dot_nn(d.astype(BF16), y_ref[every, :]))


def write_payload(out_ref, value, block):
    out_ref[block, :] = value.astype(BF16)


def write_ids(out_ref, rel_ref):
    rows = out_ref.shape[0] - ID_ROWS
    lane = lax.broadcasted_iota(jnp.int32, (ID_ROWS, out_ref.shape[1]), 1)
    ids = jnp.zeros(lane.shape, jnp.int32)
    for b in range(rel_ref.shape[0]):
        ids = jnp.where(lane == b, rel_ref[b], ids)
    out_ref[pl.ds(rows, ID_ROWS), :] = ids.astype(F32).astype(BF16)


def read_ids(payload_ref, count):
    rows = payload_ref.shape[0] - ID_ROWS
    ids = payload_ref[pl.ds(rows, ID_ROWS), :].astype(F32)
    lane = lax.broadcasted_iota(jnp.int32, ids.shape, 1)
    return [jnp.max(jnp.where(lane == b, ids, 0.0)).astype(jnp.int32) for b in range(count)]


def prepare_kernel(rel_ref, e_ref, out_ref):
    write_payload(out_ref, e_ref[...], pl.ds(0, e_ref.shape[0]))
    write_ids(out_ref, rel_ref)


def round_kernel(first, last, *refs):
    refs = list(refs)
    rel_ref = refs.pop(0)
    next_ref = None if last else refs.pop(0)
    e_ref, l_ref, r_ref, table_ref = refs[:4]
    refs = refs[4:]
    history = [refs.pop(0) for _ in range(3 * (ROUNDS - 1))] if last else None
    e_out_ref = refs.pop(0)
    if last:
        g_out_ref = refs.pop(0)
    else:
        l_out_ref, dq_ref = refs[:2]
        refs = refs[2:]
    ops_ref = refs.pop(0) if first else table_ref
    q_ref, q_far_ref, s_ref = refs[:3]
    if last:
        dq_ref, g_ref = refs[3:]
    rows = e_ref.shape[0]
    blocks = rel_ref.shape[0]
    size = rows // blocks
    if first:
        ops_ref[...] = table_ref[...].astype(BF16)
    rel_far = read_ids(r_ref, blocks)
    for b in range(blocks):
        block = pl.ds(b * size, size)
        q_ref[block, :] = dot_nn(l_ref[block, :], ops_ref[rel_ref[b]]).astype(BF16)
        q_far_ref[block, :] = dot_nn(r_ref[block, :], ops_ref[rel_far[b]]).astype(BF16)

    def own(i, value):
        dq_ref[pl.ds(i * CHUNK, CHUNK), :] = value.astype(BF16)

    two_way_gradient(q_ref, r_ref, s_ref, rows, own)
    for b in range(blocks):
        block = pl.ds(b * size, size)
        e_out_ref[block, :] = dot_nt(dq_ref[block, :], ops_ref[rel_ref[b]])

    def far(i, value):
        block = pl.ds(i * CHUNK, CHUNK)
        moved = e_ref[block, :] - embed_rate * (e_out_ref[block, :] + value.astype(BF16).astype(F32))
        e_out_ref[block, :] = moved
        if not last:
            write_payload(l_out_ref, moved, block)

    two_way_gradient(l_ref, q_far_ref, s_ref, rows, far)
    if not last:
        write_ids(l_out_ref, next_ref)
        return
    g_ref[...] = jnp.zeros(g_ref.shape, F32)
    for ids, left, grad in [history[k : k + 3] for k in range(0, len(history), 3)] + [
        (rel_ref, l_ref, dq_ref)
    ]:
        for b in range(blocks):
            block = pl.ds(b * size, size)
            g_ref[ids[b]] += dot_tn(left[block, :], grad[block, :])
    g_out_ref[...] = g_ref[...].astype(BF16)


def run_round(index, relations, e, left, right, table, history):
    first, last = index == 0, index == ROUNDS - 1
    rows, width = e.shape
    vmem = pl.BlockSpec(memory_space=pltpu.VMEM)
    smem = pl.BlockSpec(memory_space=pltpu.SMEM)
    args = [relations[index]] + ([] if last else [relations[index + 1]])
    specs = [smem] * len(args)
    args += [e, left, right, table]
    specs += [vmem] * 4
    shapes = [jax.ShapeDtypeStruct(e.shape, F32)]
    scratch = [pltpu.VMEM((rows, width), BF16)] * 2 + [pltpu.VMEM((rows, rows), F32)]
    if last:
        for k, (old_left, old_grad) in enumerate(history):
            args += [relations[k], old_left, old_grad]
            specs += [smem, vmem, vmem]
        shapes.append(jax.ShapeDtypeStruct(table.shape, BF16))
        scratch += [pltpu.VMEM((rows, width), BF16), pltpu.VMEM(table.shape, F32)]
    else:
        shapes += [jax.ShapeDtypeStruct(left.shape, BF16), jax.ShapeDtypeStruct(e.shape, BF16)]
    if first:
        shapes.append(jax.ShapeDtypeStruct(table.shape, BF16))
    return pl.pallas_call(
        functools.partial(round_kernel, first, last),
        out_shape=tuple(shapes),
        in_specs=specs,
        out_specs=(vmem,) * len(shapes),
        scratch_shapes=scratch,
        compiler_params=pltpu.CompilerParams(vmem_limit_bytes=44 * 2**20),
    )(*args)


def prepare(rel, e):
    rows, width = e.shape
    return pl.pallas_call(
        prepare_kernel,
        out_shape=jax.ShapeDtypeStruct((rows + ID_ROWS, width), BF16),
        in_specs=[pl.BlockSpec(memory_space=pltpu.SMEM), pl.BlockSpec(memory_space=pltpu.VMEM)],
        out_specs=pl.BlockSpec(memory_space=pltpu.VMEM),
    )(rel, e)


def fetch(values, mask):
    count = lax.axis_size(AXES)

    def pick(known, bit):
        if bit == 0:
            route = [(i, i ^ known) for i in range(count)]
            return lambda x: lax.ppermute(x, AXES, route)
        half = 1 << (bit - 1)
        high, low = pick(known | half, bit - 1), pick(known, bit - 1)
        return lambda x: lax.cond((mask & half) != 0, high, low, x)

    return pick(0, count.bit_length() - 1)(values)


def reduce_operators(g):
    slots = g.shape[0]
    width = g.shape[2]
    chips = lax.axis_size("chip")
    core = lax.axis_index("core")
    halves = g.reshape(2, slots // 2, width, width)
    kept = lax.dynamic_index_in_dim(halves, core, 0, keepdims=False)
    given = lax.dynamic_index_in_dim(halves, 1 - core, 0, keepdims=False)
    swap = [(0, 1), (1, 0)]
    pair = (kept.astype(F32) + lax.ppermute(given, "core", swap).astype(F32)).astype(BF16)
    parts = lax.all_to_all(pair.reshape(chips, -1, width), "chip", 0, 0, tiled=True)
    mine = jnp.sum(parts.astype(F32), axis=0, keepdims=True).astype(BF16)
    half = lax.all_to_all(jnp.broadcast_to(mine, parts.shape), "chip", 0, 0, tiled=True)
    half = half.reshape(slots // 2, width, width)
    other = lax.ppermute(half, "core", swap)
    return jnp.concatenate([jnp.where(core == 0, half, other), jnp.where(core == 0, other, half)])


def shards(embeddings, operators, plan, relations):
    e, table, history = embeddings, operators, []
    left = prepare(relations[0], e)
    for r in range(ROUNDS):
        right = fetch(left, plan[r])
        out = run_round(r, relations, e, left, right, table, history)
        if r == ROUNDS - 1:
            e, g = out
            break
        history.append((left, out[2]))
        e, left = out[:2]
        if r == 0:
            table = out[3]
    return (e, operators - operator_rate * reduce_operators(g).astype(F32))


def solution(mesh):
    pairs = jax.sharding.Mesh(mesh.devices.reshape(-1, 2), AXES)
    return jax.shard_map(
        shards,
        mesh=pairs,
        in_specs=(P(AXES, None), P(), P(), P(None, AXES)),
        out_specs=(P(AXES, None), P()),
        check_vma=False,
    )
```

```python
import functools
import math

import jax
import jax.numpy as jnp
from jax import lax
from jax.experimental import pallas as pl
from jax.experimental.pallas import tpu as pltpu
from jax.sharding import PartitionSpec as P

ROUNDS = 4
AXES = ("chip", "core")
ID_ROWS = 16
CHUNK = 256
F32 = jnp.float32
BF16 = jnp.bfloat16

embed_rate = 1.0
operator_rate = 0.02


def dot_nt(a, b):
    return lax.dot_general(a, b, (((1,), (1,)), ((), ())), preferred_element_type=F32)


def dot_nn(a, b):
    return lax.dot_general(a, b, (((1,), (0,)), ((), ())), preferred_element_type=F32)


def dot_tn(a, b):
    return lax.dot_general(a, b, (((0,), (0,)), ((), ())), preferred_element_type=F32)


def two_way_gradient(x_ref, y_ref, s_ref, rows, emit):
    width = x_ref.shape[1]
    every = pl.ds(0, rows)
    chunks = rows // CHUNK
    scale = 1.0 / math.sqrt(width)
    in_bits = scale * math.log2(math.e)
    shift = -math.log2(scale)
    row_norm = []
    col_max = col_sum = None
    for i in range(chunks):
        block = pl.ds(i * CHUNK, CHUNK)
        s = dot_nt(x_ref[block, :], y_ref[every, :]) * in_bits
        s_ref[block, :] = s
        row_max = jnp.max(s, axis=1, keepdims=True)
        row_sum = jnp.sum(jnp.exp2(s - row_max), axis=1, keepdims=True)
        row_norm.append(row_max + (jnp.log2(row_sum) + shift))
        here_max = jnp.max(s, axis=0, keepdims=True)
        if i == 0:
            col_max = here_max
            col_sum = jnp.sum(jnp.exp2(s - col_max), axis=0, keepdims=True)
        else:
            new_max = jnp.maximum(col_max, here_max)
            col_sum = col_sum * jnp.exp2(col_max - new_max) + jnp.sum(
                jnp.exp2(s - new_max), axis=0, keepdims=True
            )
            col_max = new_max
    col_norm = col_max + (jnp.log2(col_sum) + shift)
    for i in range(chunks):
        block = pl.ds(i * CHUNK, CHUNK)
        s = s_ref[block, :]
        d = jnp.exp2(s - row_norm[i]) + jnp.exp2(s - col_norm)
        at = lax.broadcasted_iota(jnp.int32, d.shape, 0) + i * CHUNK
        d = jnp.where(at == lax.broadcasted_iota(jnp.int32, d.shape, 1), d - 2.0 * scale, d)
        emit(i, dot_nn(d.astype(BF16), y_ref[every, :]))


def write_payload(out_ref, value, block):
    out_ref[block, :] = value.astype(BF16)


def write_ids(out_ref, rel_ref, index):
    rows = out_ref.shape[0] - ID_ROWS
    lane = lax.broadcasted_iota(jnp.int32, (ID_ROWS, out_ref.shape[1]), 1)
    ids = jnp.zeros(lane.shape, jnp.int32)
    for b in range(rel_ref.shape[1]):
        ids = jnp.where(lane == b, rel_ref[index, b], ids)
    out_ref[pl.ds(rows, ID_ROWS), :] = ids.astype(F32).astype(BF16)


def read_ids(payload_ref, count):
    rows = payload_ref.shape[0] - ID_ROWS
    ids = payload_ref[pl.ds(rows, ID_ROWS), :].astype(F32)
    lane = lax.broadcasted_iota(jnp.int32, ids.shape, 1)
    return [jnp.max(jnp.where(lane == b, ids, 0.0)).astype(jnp.int32) for b in range(count)]


def prepare_kernel(rel_ref, e_ref, out_ref):
    write_payload(out_ref, e_ref[...], pl.ds(0, e_ref.shape[0]))
    write_ids(out_ref, rel_ref, 0)


def round_kernel(index, *refs):
    first, last = index == 0, index == ROUNDS - 1
    refs = list(refs)
    rel_ref = refs.pop(0)
    e_ref, l_ref, r_ref, table_ref = refs[:4]
    refs = refs[4:]
    history = [refs.pop(0) for _ in range(2 * (ROUNDS - 1))] if last else None
    e_out_ref = refs.pop(0)
    if last:
        g_out_ref = refs.pop(0)
    else:
        l_out_ref, dq_ref = refs[:2]
        refs = refs[2:]
    ops_ref = refs.pop(0) if first else table_ref
    q_ref, q_far_ref, s_ref = refs[:3]
    if last:
        dq_ref, g_ref = refs[3:]
    rows = e_ref.shape[0]
    blocks = rel_ref.shape[1]
    size = rows // blocks
    if first:
        ops_ref[...] = table_ref[...].astype(BF16)
    rel_far = read_ids(r_ref, blocks)
    for b in range(blocks):
        block = pl.ds(b * size, size)
        q_ref[block, :] = dot_nn(l_ref[block, :], ops_ref[rel_ref[index, b]]).astype(BF16)
        q_far_ref[block, :] = dot_nn(r_ref[block, :], ops_ref[rel_far[b]]).astype(BF16)

    def own(i, value):
        dq_ref[pl.ds(i * CHUNK, CHUNK), :] = value.astype(BF16)

    two_way_gradient(q_ref, r_ref, s_ref, rows, own)
    for b in range(blocks):
        block = pl.ds(b * size, size)
        e_out_ref[block, :] = dot_nt(dq_ref[block, :], ops_ref[rel_ref[index, b]])

    def far(i, value):
        block = pl.ds(i * CHUNK, CHUNK)
        moved = e_ref[block, :] - embed_rate * (e_out_ref[block, :] + value.astype(BF16).astype(F32))
        e_out_ref[block, :] = moved
        if not last:
            write_payload(l_out_ref, moved, block)

    two_way_gradient(l_ref, q_far_ref, s_ref, rows, far)
    if not last:
        write_ids(l_out_ref, rel_ref, index + 1)
        return
    g_ref[...] = jnp.zeros(g_ref.shape, F32)
    history += [l_ref, dq_ref]
    for k in range(ROUNDS):
        left, grad = history[2 * k : 2 * k + 2]
        for b in range(blocks):
            block = pl.ds(b * size, size)
            g_ref[rel_ref[k, b]] += dot_tn(left[block, :], grad[block, :])
    g_out_ref[...] = g_ref[...].astype(BF16)


def run_round(index, relations, e, left, right, table, history):
    first, last = index == 0, index == ROUNDS - 1
    rows, width = e.shape
    vmem = pl.BlockSpec(memory_space=pltpu.VMEM)
    smem = pl.BlockSpec(memory_space=pltpu.SMEM)
    args = [relations, e, left, right, table]
    specs = [smem] + [vmem] * 4
    shapes = [jax.ShapeDtypeStruct(e.shape, F32)]
    scratch = [pltpu.VMEM((rows, width), BF16)] * 2 + [pltpu.VMEM((rows, rows), F32)]
    if last:
        for old in history:
            args += old
            specs += [vmem, vmem]
        shapes.append(jax.ShapeDtypeStruct(table.shape, BF16))
        scratch += [pltpu.VMEM((rows, width), BF16), pltpu.VMEM(table.shape, F32)]
    else:
        shapes += [jax.ShapeDtypeStruct(left.shape, BF16), jax.ShapeDtypeStruct(e.shape, BF16)]
    if first:
        shapes.append(jax.ShapeDtypeStruct(table.shape, BF16))
    return pl.pallas_call(
        functools.partial(round_kernel, index),
        out_shape=tuple(shapes),
        in_specs=specs,
        out_specs=(vmem,) * len(shapes),
        scratch_shapes=scratch,
        compiler_params=pltpu.CompilerParams(vmem_limit_bytes=28 * 2**20),
    )(*args)


def prepare(rel, e):
    rows, width = e.shape
    return pl.pallas_call(
        prepare_kernel,
        out_shape=jax.ShapeDtypeStruct((rows + ID_ROWS, width), BF16),
        in_specs=[pl.BlockSpec(memory_space=pltpu.SMEM), pl.BlockSpec(memory_space=pltpu.VMEM)],
        out_specs=pl.BlockSpec(memory_space=pltpu.VMEM),
    )(rel, e)


def crossing(values, mask, places, whole=None):
    count = lax.axis_size(AXES)

    def send(known):
        route = [(i, i ^ known) for i in range(count)]
        return lambda x: lax.ppermute(x, AXES, route)

    def pick(known, left):
        if not left:
            if whole is not None and known == sum(1 << p for p in places):
                return lambda x: lax.cond(mask == whole, send(whole), send(known), x)
            return send(known)
        half = 1 << left[0]
        high, low = pick(known | half, left[1:]), pick(known, left[1:])
        return lambda x: lax.cond((mask & half) != 0, high, low, x)

    return pick(0, places)(values)


def fetch(values, mask):
    bits = lax.axis_size(AXES).bit_length() - 1
    split = bits - 2
    full = (1 << bits) - 1
    values = crossing(values, mask, list(range(split))[::-1], full)
    rest = jnp.where(mask == full, 0, mask)
    return crossing(values, rest, [bits - 1, bits - 2])


def reduce_operators(g):
    slots = g.shape[0]
    width = g.shape[2]
    chips = lax.axis_size("chip")
    core = lax.axis_index("core")
    halves = g.reshape(2, slots // 2, width, width)
    kept = lax.dynamic_index_in_dim(halves, core, 0, keepdims=False)
    given = lax.dynamic_index_in_dim(halves, 1 - core, 0, keepdims=False)
    swap = [(0, 1), (1, 0)]
    pair = (kept.astype(F32) + lax.ppermute(given, "core", swap).astype(F32)).astype(BF16)
    parts = lax.all_to_all(pair.reshape(chips, -1, width), "chip", 0, 0, tiled=True)
    mine = jnp.sum(parts.astype(F32), axis=0, keepdims=True).astype(BF16)
    half = lax.all_to_all(jnp.broadcast_to(mine, parts.shape), "chip", 0, 0, tiled=True)
    half = half.reshape(slots // 2, width, width)
    other = lax.ppermute(half, "core", swap)
    return jnp.concatenate([jnp.where(core == 0, half, other), jnp.where(core == 0, other, half)])


def shards(embeddings, operators, plan, relations):
    e, table, history = embeddings, operators, []
    left = prepare(relations, e)
    for r in range(ROUNDS):
        right = fetch(left, plan[r])
        out = run_round(r, relations, e, left, right, table, history)
        if r == ROUNDS - 1:
            e, g = out
            break
        history.append((left, out[2]))
        e, left = out[:2]
        if r == 0:
            table = out[3]
    return (e, operators - operator_rate * reduce_operators(g).astype(F32))


def solution(mesh):
    pairs = jax.sharding.Mesh(mesh.devices.reshape(-1, 2), AXES)
    return jax.shard_map(
        shards,
        mesh=pairs,
        in_specs=(P(AXES, None), P(), P(), P(None, AXES)),
        out_specs=(P(AXES, None), P()),
        check_vma=False,
    )
```

```python
import functools
import math

import jax
import jax.numpy as jnp
from jax import lax
from jax.experimental import pallas as pl
from jax.experimental.pallas import tpu as pltpu
from jax.sharding import PartitionSpec as P

ROUNDS = 4
AXES = ("chip", "core")
ID_ROWS = 16
CHUNK = 256
SMALL = 128
F32 = jnp.float32
BF16 = jnp.bfloat16

embed_rate = 1.0
operator_rate = 0.02


def dot_nt(a, b):
    return lax.dot_general(a, b, (((1,), (1,)), ((), ())), preferred_element_type=F32)


def dot_nn(a, b):
    return lax.dot_general(a, b, (((1,), (0,)), ((), ())), preferred_element_type=F32)


def dot_tn(a, b):
    return lax.dot_general(a, b, (((0,), (0,)), ((), ())), preferred_element_type=F32)


def rows_at(i, size):
    return pl.ds(pl.multiple_of(i * size, size), size)


def general_gradient(k, x_ref, y_ref, s_ref, norm_ref, out_ref):
    rows, width = x_ref.shape[1:]
    scale = 1.0 / math.sqrt(width)
    in_bits = scale * math.log2(math.e)
    shift = -math.log2(scale)

    def scores(i, carry):
        col_max, col_sum = carry
        block = rows_at(i, SMALL)
        s = dot_nt(x_ref[k, block, :], y_ref[k]) * in_bits
        s_ref[block, :] = s
        row_max = jnp.max(s, axis=1, keepdims=True)
        row_sum = jnp.sum(jnp.exp2(s - row_max), axis=1, keepdims=True)
        norm_ref[block, :] = row_max + (jnp.log2(row_sum) + shift)
        new_max = jnp.maximum(col_max, jnp.max(s, axis=0, keepdims=True))
        col_sum = col_sum * jnp.exp2(col_max - new_max) + jnp.sum(
            jnp.exp2(s - new_max), axis=0, keepdims=True
        )
        return new_max, col_sum

    start = (jnp.full((1, rows), -jnp.inf, F32), jnp.zeros((1, rows), F32))
    col_max, col_sum = lax.fori_loop(0, rows // SMALL, scores, start)
    col_norm = col_max + (jnp.log2(col_sum) + shift)

    def gradient(i, carry):
        block = rows_at(i, SMALL)
        s = s_ref[block, :]
        d = jnp.exp2(s - norm_ref[block, :]) + jnp.exp2(s - col_norm)
        at = lax.broadcasted_iota(jnp.int32, d.shape, 0) + i * SMALL
        d = jnp.where(at == lax.broadcasted_iota(jnp.int32, d.shape, 1), d - 2.0 * scale, d)
        out_ref[k, block, :] = dot_nn(d.astype(BF16), y_ref[k]).astype(BF16)
        return carry

    lax.fori_loop(0, rows // SMALL, gradient, 0)


def two_way_gradient(k, x_ref, y_ref, s_ref, norm_ref, out_ref):
    rows, width = x_ref.shape[1:]
    chunks = rows // CHUNK
    scale = 1.0 / math.sqrt(width)
    in_bits = scale * math.log2(math.e)
    row_parts = []
    col_sum = jnp.zeros((1, rows), F32)
    low = high = None
    for i in range(chunks):
        block = pl.ds(i * CHUNK, CHUNK)
        e = jnp.exp2(dot_nt(x_ref[k, block, :], y_ref[k]) * in_bits)
        s_ref[block, :] = e
        row_sum = jnp.sum(e, axis=1, keepdims=True)
        col_sum = col_sum + jnp.sum(e, axis=0, keepdims=True)
        row_parts.append(scale / row_sum)
        low = row_sum if i == 0 else jnp.minimum(low, row_sum)
        high = row_sum if i == 0 else jnp.maximum(high, row_sum)
    col_part = scale / col_sum
    least = jnp.minimum(jnp.min(low), jnp.min(col_sum))
    most = jnp.maximum(jnp.max(high), jnp.max(col_sum))
    inside = jnp.logical_and(least > 2.0**-80, most < 2.0**100)

    @pl.when(inside)
    def _():
        square = (CHUNK, CHUNK)
        same = lax.broadcasted_iota(jnp.int32, square, 0) == lax.broadcasted_iota(jnp.int32, square, 1)
        diagonal = jnp.where(same, 2.0 * scale, 0.0)
        for i in range(chunks):
            block = pl.ds(i * CHUNK, CHUNK)
            strips = []
            for j in range(chunks):
                span = slice(j * CHUNK, (j + 1) * CHUNK)
                d = s_ref[block, span] * (row_parts[i] + col_part[:, span])
                strips.append((d - diagonal if i == j else d).astype(BF16))
            d = jnp.concatenate(strips, axis=1)
            out_ref[k, block, :] = dot_nn(d, y_ref[k]).astype(BF16)

    @pl.when(jnp.logical_not(inside))
    def _():
        general_gradient(k, x_ref, y_ref, s_ref, norm_ref, out_ref)


def write_payload(out_ref, value, block):
    out_ref[block, :] = value.astype(BF16)


def write_ids(out_ref, rel_ref, index):
    rows = out_ref.shape[0] - ID_ROWS
    lane = lax.broadcasted_iota(jnp.int32, (ID_ROWS, out_ref.shape[1]), 1)
    ids = jnp.zeros(lane.shape, jnp.int32)
    for b in range(rel_ref.shape[1]):
        ids = jnp.where(lane == b, rel_ref[index, b], ids)
    out_ref[pl.ds(rows, ID_ROWS), :] = ids.astype(F32).astype(BF16)


def read_ids(ids_in_ref, ids_ref):
    ids = ids_in_ref[...].astype(F32)
    lane = lax.broadcasted_iota(jnp.int32, ids.shape, 1)
    for b in range(ids_ref.shape[0]):
        ids_ref[b] = jnp.max(jnp.where(lane == b, ids, 0.0)).astype(jnp.int32)


def prepare_kernel(rel_ref, e_ref, out_ref):
    write_payload(out_ref, e_ref[...], pl.ds(0, e_ref.shape[0]))
    write_ids(out_ref, rel_ref, 0)


def round_kernel(index, *refs):
    first, last = index == 0, index == ROUNDS - 1
    refs = list(refs)
    rel_ref, e_ref, l_ref, r_ref, table_ref = refs[:5]
    refs = refs[5:]
    old = [refs.pop(0) for _ in range(2 * index if last else 0)]
    e_out_ref = refs.pop(0)
    if last:
        g_out_ref = refs.pop(0)
    else:
        l_out_ref, dq_ref = refs[:2]
        refs = refs[2:]
    ops_ref = refs.pop(0) if first else table_ref
    x_ref, y_ref, out_ref, s_ref, norm_ref, ids_ref, ids_in_ref, moved_ref, send_ref, sems = refs[:10]
    rows = moved_ref.shape[0]
    blocks = rel_ref.shape[1]
    size = rows // blocks
    every = pl.ds(0, rows)
    copies = []

    def copy(source, target):
        copies.append(pltpu.make_async_copy(source, target, sems.at[len(copies)]))
        copies[-1].start()
        return copies[-1]

    arrive = [
        copy(r_ref.at[pl.ds(rows, ID_ROWS)], ids_in_ref),
        copy(l_ref.at[every], x_ref.at[1]),
        copy(r_ref.at[every], y_ref.at[0]),
    ]
    embed_copy = copy(e_ref, moved_ref)
    if last:
        g_ref, kept_ref = refs[10:]
        arrive_old = [
            copy(old[k].at[every], kept_ref.at[k]) for k in range(2 * index)
        ]
    if first:
        for c in range(table_ref.shape[0]):
            ops_ref[c] = table_ref[c].astype(BF16)
    for one in arrive:
        one.wait()
    read_ids(ids_in_ref, ids_ref)
    for b in range(blocks):
        block = pl.ds(b * size, size)
        x_ref[0, block, :] = dot_nn(x_ref[1, block, :], ops_ref[rel_ref[index, b]]).astype(BF16)
        y_ref[1, block, :] = dot_nn(y_ref[0, block, :], ops_ref[ids_ref[b]]).astype(BF16)
    leave = []
    two_way_gradient(0, x_ref, y_ref, s_ref, norm_ref, out_ref)
    if not last:
        leave.append(copy(out_ref.at[0], dq_ref))
    two_way_gradient(1, x_ref, y_ref, s_ref, norm_ref, out_ref)
    embed_copy.wait()
    half = rows // 2
    for b in range(blocks):
        block = pl.ds(b * size, size)
        own = dot_nt(out_ref[0, block, :], ops_ref[rel_ref[index, b]])
        moved = moved_ref[block, :] - embed_rate * (own + out_ref[1, block, :].astype(F32))
        moved_ref[block, :] = moved
        if not last:
            send_ref[block, :] = moved.astype(BF16)
        if (b + 1) * size % half == 0:
            part = pl.ds((b + 1) * size - half, half)
            if not last:
                leave.append(copy(send_ref.at[part], l_out_ref.at[part]))
            leave.append(copy(moved_ref.at[part], e_out_ref.at[part]))
    if last:
        for one in arrive_old:
            one.wait()
        g_ref[...] = jnp.zeros(g_ref.shape, F32)
        for k in range(ROUNDS):
            for b in range(blocks):
                block = pl.ds(b * size, size)
                left = x_ref[1, block, :] if k == index else kept_ref[2 * k, block, :]
                grad = out_ref[0, block, :] if k == index else kept_ref[2 * k + 1, block, :]
                g_ref[rel_ref[k, b]] += dot_tn(left, grad)
        for c in range(g_ref.shape[0]):
            g_out_ref[c] = g_ref[c].astype(BF16)
    else:
        write_ids(send_ref, rel_ref, index + 1)
        tail = pl.ds(rows, ID_ROWS)
        leave.append(copy(send_ref.at[tail], l_out_ref.at[tail]))
    for one in leave:
        one.wait()


def run_round(index, relations, e, left, right, table, history):
    first, last = index == 0, index == ROUNDS - 1
    rows, width = e.shape
    vmem = pl.BlockSpec(memory_space=pltpu.VMEM)
    hbm = pl.BlockSpec(memory_space=pltpu.HBM)
    args = [relations, e, left, right, table]
    specs = [pl.BlockSpec(memory_space=pltpu.SMEM)] + [hbm] * 3 + [vmem]
    shapes = [jax.ShapeDtypeStruct(e.shape, F32)]
    outs = [hbm]
    scratch = [pltpu.VMEM((2, rows, width), BF16)] * 3 + [
        pltpu.VMEM((rows, rows), F32),
        pltpu.VMEM((rows, 1), F32),
        pltpu.SMEM((relations.shape[1],), jnp.int32),
        pltpu.VMEM((ID_ROWS, width), BF16),
        pltpu.VMEM((rows, width), F32),
        pltpu.VMEM((rows + ID_ROWS, width), BF16),
        pltpu.SemaphoreType.DMA((16,)),
    ]
    if last:
        for old in history:
            args += old
            specs += [hbm] * 2
        shapes.append(jax.ShapeDtypeStruct(table.shape, BF16))
        outs.append(vmem)
        scratch += [pltpu.VMEM(table.shape, F32), pltpu.VMEM((2 * index, rows, width), BF16)]
    else:
        shapes += [jax.ShapeDtypeStruct(left.shape, BF16), jax.ShapeDtypeStruct(e.shape, BF16)]
        outs += [hbm] * 2
    if first:
        shapes.append(jax.ShapeDtypeStruct(table.shape, BF16))
        outs.append(vmem)
    return pl.pallas_call(
        functools.partial(round_kernel, index),
        out_shape=tuple(shapes),
        in_specs=specs,
        out_specs=tuple(outs),
        scratch_shapes=scratch,
        compiler_params=pltpu.CompilerParams(vmem_limit_bytes=60 * 2**20),
    )(*args)


def prepare(rel, e):
    rows, width = e.shape
    return pl.pallas_call(
        prepare_kernel,
        out_shape=jax.ShapeDtypeStruct((rows + ID_ROWS, width), BF16),
        in_specs=[pl.BlockSpec(memory_space=pltpu.SMEM), pl.BlockSpec(memory_space=pltpu.VMEM)],
        out_specs=pl.BlockSpec(memory_space=pltpu.VMEM),
    )(rel, e)


def keep(values):
    def kernel(in_ref, out_ref):
        out_ref[...] = in_ref[...]

    spec = pl.BlockSpec(memory_space=pltpu.VMEM)
    shape = jax.ShapeDtypeStruct(values.shape, values.dtype)
    return pl.pallas_call(kernel, out_shape=shape, in_specs=[spec], out_specs=spec)(values)


def crossing(values, mask, places, whole=None):
    count = lax.axis_size(AXES)

    def send(known):
        if known == 0:
            return keep
        route = [(i, i ^ known) for i in range(count)]
        return lambda x: lax.ppermute(x, AXES, route)

    def pick(known, left):
        if not left:
            if whole is not None and known == sum(1 << p for p in places):
                return lambda x: lax.cond(mask == whole, send(whole), send(known), x)
            return send(known)
        half = 1 << left[0]
        high, low = pick(known | half, left[1:]), pick(known, left[1:])
        return lambda x: lax.cond((mask & half) != 0, high, low, x)

    return pick(0, places)(values)


def fetch(values, mask):
    bits = lax.axis_size(AXES).bit_length() - 1
    split = bits - 2
    full = (1 << bits) - 1
    values = crossing(values, mask, list(range(split))[::-1], full)
    rest = jnp.where(mask == full, 0, mask)
    return crossing(values, rest, [bits - 1, bits - 2])


def reduce_operators(g):
    slots = g.shape[0]
    width = g.shape[2]
    chips = lax.axis_size("chip")
    core = lax.axis_index("core")
    halves = g.reshape(2, slots // 2, width, width)
    kept = lax.dynamic_index_in_dim(halves, core, 0, keepdims=False)
    given = lax.dynamic_index_in_dim(halves, 1 - core, 0, keepdims=False)
    swap = [(0, 1), (1, 0)]
    pair = (kept.astype(F32) + lax.ppermute(given, "core", swap).astype(F32)).astype(BF16)
    parts = lax.all_to_all(pair.reshape(chips, -1, width), "chip", 0, 0, tiled=True)
    mine = jnp.sum(parts.astype(F32), axis=0, keepdims=True).astype(BF16)
    half = lax.all_to_all(jnp.broadcast_to(mine, parts.shape), "chip", 0, 0, tiled=True)
    half = half.reshape(slots // 2, width, width)
    other = lax.ppermute(half, "core", swap)
    return jnp.concatenate([jnp.where(core == 0, half, other), jnp.where(core == 0, other, half)])


def shards(embeddings, operators, plan, relations):
    e, table, history = embeddings, operators, []
    left = prepare(relations, e)
    for r in range(ROUNDS):
        right = fetch(left, plan[r])
        out = run_round(r, relations, e, left, right, table, history)
        if r == ROUNDS - 1:
            e, g = out
            break
        history.append((left, out[2]))
        e, left = out[:2]
        if r == 0:
            table = out[3]
    return (e, operators - operator_rate * reduce_operators(g).astype(F32))


def solution(mesh):
    pairs = jax.sharding.Mesh(mesh.devices.reshape(-1, 2), AXES)
    return jax.shard_map(
        shards,
        mesh=pairs,
        in_specs=(P(AXES, None), P(), P(), P(None, AXES)),
        out_specs=(P(AXES, None), P()),
        check_vma=False,
    )
```

```python
import functools
import math

import jax
import jax.numpy as jnp
from jax import lax
from jax.experimental import pallas as pl
from jax.experimental.pallas import tpu as pltpu
from jax.sharding import PartitionSpec as P

ROUNDS = 4
AXES = ("chip", "core")
ID_ROWS = 16
CHUNK = 256
SMALL = 128
F32 = jnp.float32
BF16 = jnp.bfloat16

embed_rate = 1.0
operator_rate = 0.02


def dot_nt(a, b):
    return lax.dot_general(a, b, (((1,), (1,)), ((), ())), preferred_element_type=F32)


def dot_nn(a, b):
    return lax.dot_general(a, b, (((1,), (0,)), ((), ())), preferred_element_type=F32)


def dot_tn(a, b):
    return lax.dot_general(a, b, (((0,), (0,)), ((), ())), preferred_element_type=F32)


def rows_at(i, size):
    return pl.ds(pl.multiple_of(i * size, size), size)


def general_gradient(k, x_ref, y_ref, s_ref, norm_ref, out_ref):
    rows, width = x_ref.shape[1:]
    scale = 1.0 / math.sqrt(width)
    in_bits = scale * math.log2(math.e)
    shift = -math.log2(scale)

    def scores(i, carry):
        col_max, col_sum = carry
        block = rows_at(i, SMALL)
        s = dot_nt(x_ref[k, block, :], y_ref[k]) * in_bits
        s_ref[block, :] = s
        row_max = jnp.max(s, axis=1, keepdims=True)
        row_sum = jnp.sum(jnp.exp2(s - row_max), axis=1, keepdims=True)
        norm_ref[block, :] = row_max + (jnp.log2(row_sum) + shift)
        new_max = jnp.maximum(col_max, jnp.max(s, axis=0, keepdims=True))
        col_sum = col_sum * jnp.exp2(col_max - new_max) + jnp.sum(
            jnp.exp2(s - new_max), axis=0, keepdims=True
        )
        return new_max, col_sum

    start = (jnp.full((1, rows), -jnp.inf, F32), jnp.zeros((1, rows), F32))
    col_max, col_sum = lax.fori_loop(0, rows // SMALL, scores, start)
    col_norm = col_max + (jnp.log2(col_sum) + shift)

    def gradient(i, carry):
        block = rows_at(i, SMALL)
        s = s_ref[block, :]
        d = jnp.exp2(s - norm_ref[block, :]) + jnp.exp2(s - col_norm)
        at = lax.broadcasted_iota(jnp.int32, d.shape, 0) + i * SMALL
        d = jnp.where(at == lax.broadcasted_iota(jnp.int32, d.shape, 1), d - 2.0 * scale, d)
        out_ref[k, block, :] = dot_nn(d.astype(BF16), y_ref[k]).astype(BF16)
        return carry

    lax.fori_loop(0, rows // SMALL, gradient, 0)


def two_way_gradient(k, x_ref, y_ref, s_ref, norm_ref, out_ref):
    rows, width = x_ref.shape[1:]
    chunks = rows // CHUNK
    scale = 1.0 / math.sqrt(width)
    in_bits = scale * math.log2(math.e)
    row_parts = []
    col_sum = jnp.zeros((1, rows), F32)
    low = high = None
    for i in range(chunks):
        block = pl.ds(i * CHUNK, CHUNK)
        e = jnp.exp2(dot_nt(x_ref[k, block, :], y_ref[k]) * in_bits)
        s_ref[block, :] = e
        row_sum = jnp.sum(e, axis=1, keepdims=True)
        col_sum = col_sum + jnp.sum(e, axis=0, keepdims=True)
        row_parts.append(scale / row_sum)
        low = row_sum if i == 0 else jnp.minimum(low, row_sum)
        high = row_sum if i == 0 else jnp.maximum(high, row_sum)
    col_part = scale / col_sum
    least = jnp.minimum(jnp.min(low), jnp.min(col_sum))
    most = jnp.maximum(jnp.max(high), jnp.max(col_sum))
    inside = jnp.logical_and(least > 2.0**-80, most < 2.0**100)

    @pl.when(inside)
    def _():
        square = (CHUNK, CHUNK)
        same = lax.broadcasted_iota(jnp.int32, square, 0) == lax.broadcasted_iota(jnp.int32, square, 1)
        diagonal = jnp.where(same, 2.0 * scale, 0.0)
        for i in range(chunks):
            block = pl.ds(i * CHUNK, CHUNK)
            strips = []
            for j in range(chunks):
                span = slice(j * CHUNK, (j + 1) * CHUNK)
                d = s_ref[block, span] * (row_parts[i] + col_part[:, span])
                strips.append((d - diagonal if i == j else d).astype(BF16))
            d = jnp.concatenate(strips, axis=1)
            out_ref[k, block, :] = dot_nn(d, y_ref[k]).astype(BF16)

    @pl.when(jnp.logical_not(inside))
    def _():
        general_gradient(k, x_ref, y_ref, s_ref, norm_ref, out_ref)


def write_payload(out_ref, value, block):
    out_ref[block, :] = value.astype(BF16)


def write_ids(out_ref, rel_ref, index):
    rows = out_ref.shape[0] - ID_ROWS
    lane = lax.broadcasted_iota(jnp.int32, (ID_ROWS, out_ref.shape[1]), 1)
    ids = jnp.zeros(lane.shape, jnp.int32)
    for b in range(rel_ref.shape[1]):
        ids = jnp.where(lane == b, rel_ref[index, b], ids)
    out_ref[pl.ds(rows, ID_ROWS), :] = ids.astype(F32).astype(BF16)


def read_ids(ids_in_ref, ids_ref):
    ids = ids_in_ref[...].astype(F32)
    lane = lax.broadcasted_iota(jnp.int32, ids.shape, 1)
    for b in range(ids_ref.shape[0]):
        ids_ref[b] = jnp.max(jnp.where(lane == b, ids, 0.0)).astype(jnp.int32)


def prepare_kernel(rel_ref, e_ref, out_ref):
    write_payload(out_ref, e_ref[...], pl.ds(0, e_ref.shape[0]))
    write_ids(out_ref, rel_ref, 0)


def round_kernel(index, *refs):
    first, last = index == 0, index == ROUNDS - 1
    refs = list(refs)
    rel_ref, e_ref, l_ref, r_ref, table_ref = refs[:5]
    refs = refs[5:]
    old = [refs.pop(0) for _ in range(2 * index if last else 0)]
    core_ref = refs.pop(0) if last else None
    e_out_ref = refs.pop(0)
    outputs, refs = refs[:2], refs[2:]
    if last:
        kept_out_ref, given_out_ref = outputs
    else:
        l_out_ref, dq_ref = outputs
    ops_ref = refs.pop(0) if first else table_ref
    x_ref, y_ref, out_ref, s_ref, norm_ref, ids_ref, ids_in_ref, moved_ref, send_ref, sems = refs[:10]
    rows = moved_ref.shape[0]
    blocks = rel_ref.shape[1]
    size = rows // blocks
    every = pl.ds(0, rows)
    copies = []

    def copy(source, target):
        copies.append(pltpu.make_async_copy(source, target, sems.at[len(copies)]))
        copies[-1].start()
        return copies[-1]

    arrive = [
        copy(r_ref.at[pl.ds(rows, ID_ROWS)], ids_in_ref),
        copy(l_ref.at[every], x_ref.at[1]),
        copy(r_ref.at[every], y_ref.at[0]),
    ]
    embed_copy = copy(e_ref, moved_ref)
    if last:
        g_ref, kept_ref = refs[10:]
        arrive_old = [
            copy(old[k].at[every], kept_ref.at[k]) for k in range(2 * index)
        ]
    if first:
        for c in range(table_ref.shape[0]):
            ops_ref[c] = table_ref[c].astype(BF16)
    for one in arrive:
        one.wait()
    read_ids(ids_in_ref, ids_ref)
    for b in range(blocks):
        block = pl.ds(b * size, size)
        x_ref[0, block, :] = dot_nn(x_ref[1, block, :], ops_ref[rel_ref[index, b]]).astype(BF16)
        y_ref[1, block, :] = dot_nn(y_ref[0, block, :], ops_ref[ids_ref[b]]).astype(BF16)
    leave = []
    two_way_gradient(0, x_ref, y_ref, s_ref, norm_ref, out_ref)
    if not last:
        leave.append(copy(out_ref.at[0], dq_ref))
    two_way_gradient(1, x_ref, y_ref, s_ref, norm_ref, out_ref)
    embed_copy.wait()
    half = rows // 2
    for b in range(blocks):
        block = pl.ds(b * size, size)
        own = dot_nt(out_ref[0, block, :], ops_ref[rel_ref[index, b]])
        moved = moved_ref[block, :] - embed_rate * (own + out_ref[1, block, :].astype(F32))
        moved_ref[block, :] = moved
        if not last:
            send_ref[block, :] = moved.astype(BF16)
        if (b + 1) * size % half == 0:
            part = pl.ds((b + 1) * size - half, half)
            if not last:
                leave.append(copy(send_ref.at[part], l_out_ref.at[part]))
            leave.append(copy(moved_ref.at[part], e_out_ref.at[part]))
    if last:
        for one in arrive_old:
            one.wait()
        g_ref[...] = jnp.zeros(g_ref.shape, F32)
        for k in range(ROUNDS):
            for b in range(blocks):
                block = pl.ds(b * size, size)
                left = x_ref[1, block, :] if k == index else kept_ref[2 * k, block, :]
                grad = out_ref[0, block, :] if k == index else kept_ref[2 * k + 1, block, :]
                g_ref[rel_ref[k, b]] += dot_tn(left, grad)
        half = g_ref.shape[0] // 2
        for c in range(half):
            kept_out_ref[c] = g_ref[core_ref[0] * half + c].astype(BF16)
            given_out_ref[c] = g_ref[half - core_ref[0] * half + c].astype(BF16)
    else:
        write_ids(send_ref, rel_ref, index + 1)
        tail = pl.ds(rows, ID_ROWS)
        leave.append(copy(send_ref.at[tail], l_out_ref.at[tail]))
    for one in leave:
        one.wait()


def run_round(index, relations, e, left, right, table, history):
    first, last = index == 0, index == ROUNDS - 1
    rows, width = e.shape
    vmem = pl.BlockSpec(memory_space=pltpu.VMEM)
    hbm = pl.BlockSpec(memory_space=pltpu.HBM)
    args = [relations, e, left, right, table]
    specs = [pl.BlockSpec(memory_space=pltpu.SMEM)] + [hbm] * 3 + [vmem]
    shapes = [jax.ShapeDtypeStruct(e.shape, F32)]
    outs = [hbm]
    scratch = [pltpu.VMEM((2, rows, width), BF16)] * 3 + [
        pltpu.VMEM((rows, rows), F32),
        pltpu.VMEM((rows, 1), F32),
        pltpu.SMEM((relations.shape[1],), jnp.int32),
        pltpu.VMEM((ID_ROWS, width), BF16),
        pltpu.VMEM((rows, width), F32),
        pltpu.VMEM((rows + ID_ROWS, width), BF16),
        pltpu.SemaphoreType.DMA((16,)),
    ]
    if last:
        for old in history:
            args += old
            specs += [hbm] * 2
        args.append(lax.axis_index("core").astype(jnp.int32).reshape(1))
        specs.append(pl.BlockSpec(memory_space=pltpu.SMEM))
        half = (table.shape[0] // 2,) + table.shape[1:]
        shapes += [jax.ShapeDtypeStruct(half, BF16)] * 2
        outs += [vmem] * 2
        scratch += [pltpu.VMEM(table.shape, F32), pltpu.VMEM((2 * index, rows, width), BF16)]
    else:
        shapes += [jax.ShapeDtypeStruct(left.shape, BF16), jax.ShapeDtypeStruct(e.shape, BF16)]
        outs += [hbm] * 2
    if first:
        shapes.append(jax.ShapeDtypeStruct(table.shape, BF16))
        outs.append(vmem)
    return pl.pallas_call(
        functools.partial(round_kernel, index),
        out_shape=tuple(shapes),
        in_specs=specs,
        out_specs=tuple(outs),
        scratch_shapes=scratch,
        compiler_params=pltpu.CompilerParams(vmem_limit_bytes=60 * 2**20),
    )(*args)


def prepare(rel, e):
    rows, width = e.shape
    return pl.pallas_call(
        prepare_kernel,
        out_shape=jax.ShapeDtypeStruct((rows + ID_ROWS, width), BF16),
        in_specs=[pl.BlockSpec(memory_space=pltpu.SMEM), pl.BlockSpec(memory_space=pltpu.VMEM)],
        out_specs=pl.BlockSpec(memory_space=pltpu.VMEM),
    )(rel, e)


def keep(values):
    def kernel(in_ref, out_ref, sem):
        copy = pltpu.make_async_copy(in_ref, out_ref, sem)
        copy.start()
        copy.wait()

    hbm = pl.BlockSpec(memory_space=pltpu.HBM)
    return pl.pallas_call(
        kernel,
        out_shape=jax.ShapeDtypeStruct(values.shape, values.dtype),
        in_specs=[hbm],
        out_specs=hbm,
        scratch_shapes=[pltpu.SemaphoreType.DMA],
        compiler_params=pltpu.CompilerParams(vmem_limit_bytes=60 * 2**20),
    )(values)


def crossing(values, mask, places, whole=None):
    count = lax.axis_size(AXES)

    def send(known):
        if known == 0:
            return keep
        route = [(i, i ^ known) for i in range(count)]
        return lambda x: lax.ppermute(x, AXES, route)

    def pick(known, left):
        if not left:
            if whole is not None and known == sum(1 << p for p in places):
                return lambda x: lax.cond(mask == whole, send(whole), send(known), x)
            return send(known)
        half = 1 << left[0]
        high, low = pick(known | half, left[1:]), pick(known, left[1:])
        return lambda x: lax.cond((mask & half) != 0, high, low, x)

    return pick(0, places)(values)


def fetch(values, mask):
    bits = lax.axis_size(AXES).bit_length() - 1
    full = (1 << bits) - 1
    values = crossing(values, mask, list(range(1, bits - 2))[::-1], full)
    rest = jnp.where(mask == full, 0, mask)
    values = crossing(values, rest, [bits - 1, bits - 2])
    return crossing(values, rest, [0])


def reduce_operators(kept, given):
    width = kept.shape[2]
    chips = lax.axis_size("chip")
    core = lax.axis_index("core")
    swap = [(0, 1), (1, 0)]
    pair = (kept.astype(F32) + lax.ppermute(given, "core", swap).astype(F32)).astype(BF16)
    parts = lax.all_to_all(pair.reshape(chips, -1, width), "chip", 0, 0, tiled=True)
    mine = jnp.sum(parts.astype(F32), axis=0, keepdims=True).astype(BF16)
    half = lax.all_to_all(jnp.broadcast_to(mine, parts.shape), "chip", 0, 0, tiled=True)
    half = half.reshape(kept.shape)
    other = lax.ppermute(half, "core", swap)
    return jnp.concatenate([jnp.where(core == 0, half, other), jnp.where(core == 0, other, half)])


def shards(embeddings, operators, plan, relations):
    e, table, history = embeddings, operators, []
    left = prepare(relations, e)
    for r in range(ROUNDS):
        right = fetch(left, plan[r])
        out = run_round(r, relations, e, left, right, table, history)
        if r == ROUNDS - 1:
            e, kept, given = out
            break
        history.append((left, out[2]))
        e, left = out[:2]
        if r == 0:
            table = out[3]
    return (e, operators - operator_rate * reduce_operators(kept, given).astype(F32))


def solution(mesh):
    pairs = jax.sharding.Mesh(mesh.devices.reshape(-1, 2), AXES)
    return jax.shard_map(
        shards,
        mesh=pairs,
        in_specs=(P(AXES, None), P(), P(), P(None, AXES)),
        out_specs=(P(AXES, None), P()),
        check_vma=False,
    )
```

```python
import functools
import math

import jax
import jax.numpy as jnp
from jax import lax
from jax.experimental import pallas as pl
from jax.experimental.pallas import tpu as pltpu
from jax.sharding import PartitionSpec as P

ROUNDS = 4
AXES = ("chip", "core")
ID_ROWS = 16
CHUNK = 256
SMALL = 128
F32 = jnp.float32
BF16 = jnp.bfloat16

embed_rate = 1.0
operator_rate = 0.02


def dot_nt(a, b):
    return lax.dot_general(a, b, (((1,), (1,)), ((), ())), preferred_element_type=F32)


def dot_nn(a, b):
    return lax.dot_general(a, b, (((1,), (0,)), ((), ())), preferred_element_type=F32)


def dot_tn(a, b):
    return lax.dot_general(a, b, (((0,), (0,)), ((), ())), preferred_element_type=F32)


def rows_at(i, size):
    return pl.ds(pl.multiple_of(i * size, size), size)


def general_gradient(k, x_ref, y_ref, s_ref, norm_ref, out_ref):
    rows, width = x_ref.shape[1:]
    scale = 1.0 / math.sqrt(width)
    in_bits = scale * math.log2(math.e)
    shift = -math.log2(scale)

    def scores(i, carry):
        col_max, col_sum = carry
        block = rows_at(i, SMALL)
        s = dot_nt(x_ref[k, block, :], y_ref[k]) * in_bits
        s_ref[block, :] = s
        row_max = jnp.max(s, axis=1, keepdims=True)
        row_sum = jnp.sum(jnp.exp2(s - row_max), axis=1, keepdims=True)
        norm_ref[block, :] = row_max + (jnp.log2(row_sum) + shift)
        new_max = jnp.maximum(col_max, jnp.max(s, axis=0, keepdims=True))
        col_sum = col_sum * jnp.exp2(col_max - new_max) + jnp.sum(
            jnp.exp2(s - new_max), axis=0, keepdims=True
        )
        return new_max, col_sum

    start = (jnp.full((1, rows), -jnp.inf, F32), jnp.zeros((1, rows), F32))
    col_max, col_sum = lax.fori_loop(0, rows // SMALL, scores, start)
    col_norm = col_max + (jnp.log2(col_sum) + shift)

    def gradient(i, carry):
        block = rows_at(i, SMALL)
        s = s_ref[block, :]
        d = jnp.exp2(s - norm_ref[block, :]) + jnp.exp2(s - col_norm)
        at = lax.broadcasted_iota(jnp.int32, d.shape, 0) + i * SMALL
        d = jnp.where(at == lax.broadcasted_iota(jnp.int32, d.shape, 1), d - 2.0 * scale, d)
        out_ref[k, block, :] = dot_nn(d.astype(BF16), y_ref[k]).astype(BF16)
        return carry

    lax.fori_loop(0, rows // SMALL, gradient, 0)


def two_way_gradient(k, x_ref, y_ref, s_ref, norm_ref, out_ref):
    rows, width = x_ref.shape[1:]
    chunks = rows // CHUNK
    scale = 1.0 / math.sqrt(width)
    in_bits = scale * math.log2(math.e)
    row_parts = []
    col_sum = jnp.zeros((1, rows), F32)
    low = high = None
    for i in range(chunks):
        block = pl.ds(i * CHUNK, CHUNK)
        e = jnp.exp2(dot_nt(x_ref[k, block, :], y_ref[k]) * in_bits)
        s_ref[block, :] = e
        row_sum = jnp.sum(e, axis=1, keepdims=True)
        col_sum = col_sum + jnp.sum(e, axis=0, keepdims=True)
        row_parts.append(scale / row_sum)
        low = row_sum if i == 0 else jnp.minimum(low, row_sum)
        high = row_sum if i == 0 else jnp.maximum(high, row_sum)
    col_part = scale / col_sum
    least = jnp.minimum(jnp.min(low), jnp.min(col_sum))
    most = jnp.maximum(jnp.max(high), jnp.max(col_sum))
    inside = jnp.logical_and(least > 2.0**-80, most < 2.0**100)

    @pl.when(inside)
    def _():
        square = (CHUNK, CHUNK)
        same = lax.broadcasted_iota(jnp.int32, square, 0) == lax.broadcasted_iota(jnp.int32, square, 1)
        diagonal = jnp.where(same, 2.0 * scale, 0.0)
        for i in range(chunks):
            block = pl.ds(i * CHUNK, CHUNK)
            strips = []
            for j in range(chunks):
                span = slice(j * CHUNK, (j + 1) * CHUNK)
                d = s_ref[block, span] * (row_parts[i] + col_part[:, span])
                strips.append((d - diagonal if i == j else d).astype(BF16))
            d = jnp.concatenate(strips, axis=1)
            out_ref[k, block, :] = dot_nn(d, y_ref[k]).astype(BF16)

    @pl.when(jnp.logical_not(inside))
    def _():
        general_gradient(k, x_ref, y_ref, s_ref, norm_ref, out_ref)


def write_payload(out_ref, value, block):
    out_ref[block, :] = value.astype(BF16)


def write_ids(out_ref, rel_ref, index):
    rows = out_ref.shape[0] - ID_ROWS
    lane = lax.broadcasted_iota(jnp.int32, (ID_ROWS, out_ref.shape[1]), 1)
    ids = jnp.zeros(lane.shape, jnp.int32)
    for b in range(rel_ref.shape[1]):
        ids = jnp.where(lane == b, rel_ref[index, b], ids)
    out_ref[pl.ds(rows, ID_ROWS), :] = ids.astype(F32).astype(BF16)


def read_ids(ids_in_ref, ids_ref):
    ids = ids_in_ref[...].astype(F32)
    lane = lax.broadcasted_iota(jnp.int32, ids.shape, 1)
    for b in range(ids_ref.shape[0]):
        ids_ref[b] = jnp.max(jnp.where(lane == b, ids, 0.0)).astype(jnp.int32)


def prepare_kernel(rel_ref, e_ref, out_ref):
    write_payload(out_ref, e_ref[...], pl.ds(0, e_ref.shape[0]))
    write_ids(out_ref, rel_ref, 0)


def round_kernel(index, *refs):
    first, last = index == 0, index == ROUNDS - 1
    refs = list(refs)
    rel_ref, e_ref, l_ref, r_ref, table_ref = refs[:5]
    refs = refs[5:]
    old = [refs.pop(0) for _ in range(2 * index if last else 0)]
    core_ref = refs.pop(0) if last else None
    e_out_ref = refs.pop(0)
    outputs, refs = refs[:2], refs[2:]
    if last:
        kept_out_ref, given_out_ref = outputs
    else:
        l_out_ref, dq_ref = outputs
    ops_ref = refs.pop(0) if first else table_ref
    x_ref, y_ref, out_ref, s_ref, norm_ref, ids_ref, ids_in_ref, moved_ref, send_ref, sems = refs[:10]
    rows = moved_ref.shape[0]
    blocks = rel_ref.shape[1]
    size = rows // blocks
    every = pl.ds(0, rows)
    copies = []

    def copy(source, target):
        copies.append(pltpu.make_async_copy(source, target, sems.at[len(copies)]))
        copies[-1].start()
        return copies[-1]

    arrive = [
        copy(r_ref.at[pl.ds(rows, ID_ROWS)], ids_in_ref),
        copy(l_ref.at[every], x_ref.at[1]),
        copy(r_ref.at[every], y_ref.at[0]),
    ]
    embed_copy = copy(e_ref, moved_ref)
    if last:
        g_ref, kept_ref = refs[10:]
        arrive_old = [
            copy(old[k].at[every], kept_ref.at[k]) for k in range(2 * index)
        ]
    if first:
        for c in range(table_ref.shape[0]):
            ops_ref[c] = table_ref[c].astype(BF16)
    for one in arrive:
        one.wait()
    read_ids(ids_in_ref, ids_ref)
    for b in range(blocks):
        block = pl.ds(b * size, size)
        x_ref[0, block, :] = dot_nn(x_ref[1, block, :], ops_ref[rel_ref[index, b]]).astype(BF16)
        y_ref[1, block, :] = dot_nn(y_ref[0, block, :], ops_ref[ids_ref[b]]).astype(BF16)
    leave = []
    two_way_gradient(0, x_ref, y_ref, s_ref, norm_ref, out_ref)
    if not last:
        leave.append(copy(out_ref.at[0], dq_ref))
    two_way_gradient(1, x_ref, y_ref, s_ref, norm_ref, out_ref)
    embed_copy.wait()
    half = rows // 2
    for b in range(blocks):
        block = pl.ds(b * size, size)
        own = dot_nt(out_ref[0, block, :], ops_ref[rel_ref[index, b]])
        moved = moved_ref[block, :] - embed_rate * (own + out_ref[1, block, :].astype(F32))
        moved_ref[block, :] = moved
        if not last:
            send_ref[block, :] = moved.astype(BF16)
        if (b + 1) * size % half == 0:
            part = pl.ds((b + 1) * size - half, half)
            if not last:
                leave.append(copy(send_ref.at[part], l_out_ref.at[part]))
            leave.append(copy(moved_ref.at[part], e_out_ref.at[part]))
    if last:
        for one in arrive_old:
            one.wait()
        g_ref[...] = jnp.zeros(g_ref.shape, F32)
        for k in range(ROUNDS):
            for b in range(blocks):
                block = pl.ds(b * size, size)
                left = x_ref[1, block, :] if k == index else kept_ref[2 * k, block, :]
                grad = out_ref[0, block, :] if k == index else kept_ref[2 * k + 1, block, :]
                g_ref[rel_ref[k, b]] += dot_tn(left, grad)
        half = g_ref.shape[0] // 2
        for c in range(half):
            kept_out_ref[c] = g_ref[core_ref[0] * half + c].astype(BF16)
            given_out_ref[c] = g_ref[half - core_ref[0] * half + c].astype(BF16)
    else:
        write_ids(send_ref, rel_ref, index + 1)
        tail = pl.ds(rows, ID_ROWS)
        leave.append(copy(send_ref.at[tail], l_out_ref.at[tail]))
    for one in leave:
        one.wait()


def run_round(index, relations, e, left, right, table, history):
    first, last = index == 0, index == ROUNDS - 1
    rows, width = e.shape
    vmem = pl.BlockSpec(memory_space=pltpu.VMEM)
    hbm = pl.BlockSpec(memory_space=pltpu.HBM)
    args = [relations, e, left, right, table]
    specs = [pl.BlockSpec(memory_space=pltpu.SMEM)] + [hbm] * 3 + [vmem]
    shapes = [jax.ShapeDtypeStruct(e.shape, F32)]
    outs = [hbm]
    scratch = [pltpu.VMEM((2, rows, width), BF16)] * 3 + [
        pltpu.VMEM((rows, rows), F32),
        pltpu.VMEM((rows, 1), F32),
        pltpu.SMEM((relations.shape[1],), jnp.int32),
        pltpu.VMEM((ID_ROWS, width), BF16),
        pltpu.VMEM((rows, width), F32),
        pltpu.VMEM((rows + ID_ROWS, width), BF16),
        pltpu.SemaphoreType.DMA((16,)),
    ]
    if last:
        for old in history:
            args += old
            specs += [hbm] * 2
        args.append(lax.axis_index("core").astype(jnp.int32).reshape(1))
        specs.append(pl.BlockSpec(memory_space=pltpu.SMEM))
        half = (table.shape[0] // 2,) + table.shape[1:]
        shapes += [jax.ShapeDtypeStruct(half, BF16)] * 2
        outs += [vmem] * 2
        scratch += [pltpu.VMEM(table.shape, F32), pltpu.VMEM((2 * index, rows, width), BF16)]
    else:
        shapes += [jax.ShapeDtypeStruct(left.shape, BF16), jax.ShapeDtypeStruct(e.shape, BF16)]
        outs += [hbm] * 2
    if first:
        shapes.append(jax.ShapeDtypeStruct(table.shape, BF16))
        outs.append(vmem)
    return pl.pallas_call(
        functools.partial(round_kernel, index),
        out_shape=tuple(shapes),
        in_specs=specs,
        out_specs=tuple(outs),
        scratch_shapes=scratch,
        compiler_params=pltpu.CompilerParams(vmem_limit_bytes=60 * 2**20),
    )(*args)


def prepare(rel, e):
    rows, width = e.shape
    return pl.pallas_call(
        prepare_kernel,
        out_shape=jax.ShapeDtypeStruct((rows + ID_ROWS, width), BF16),
        in_specs=[pl.BlockSpec(memory_space=pltpu.SMEM), pl.BlockSpec(memory_space=pltpu.VMEM)],
        out_specs=pl.BlockSpec(memory_space=pltpu.VMEM),
    )(rel, e)


def keep(values):
    def kernel(in_ref, out_ref):
        out_ref[...] = in_ref[...]

    spec = pl.BlockSpec(memory_space=pltpu.VMEM)
    shape = jax.ShapeDtypeStruct(values.shape, values.dtype)
    return pl.pallas_call(kernel, out_shape=shape, in_specs=[spec], out_specs=spec)(values)


def crossing(values, mask, places, whole=None):
    count = lax.axis_size(AXES)

    def send(known):
        if known == 0:
            return keep
        route = [(i, i ^ known) for i in range(count)]
        return lambda x: lax.ppermute(x, AXES, route)

    def pick(known, left):
        if not left:
            if whole is not None and known == sum(1 << p for p in places):
                return lambda x: lax.cond(mask == whole, send(whole), send(known), x)
            return send(known)
        half = 1 << left[0]
        high, low = pick(known | half, left[1:]), pick(known, left[1:])
        return lambda x: lax.cond((mask & half) != 0, high, low, x)

    return pick(0, places)(values)


def fetch(values, mask):
    bits = lax.axis_size(AXES).bit_length() - 1
    full = (1 << bits) - 1
    values = crossing(values, mask, list(range(1, bits - 2))[::-1], full)
    rest = jnp.where(mask == full, 0, mask)
    values = crossing(values, rest, [bits - 1, bits - 2])
    return crossing(values, rest, [0])


def reduce_operators(kept, given):
    width = kept.shape[2]
    chips = lax.axis_size("chip")
    core = lax.axis_index("core")
    swap = [(0, 1), (1, 0)]
    pair = (kept.astype(F32) + lax.ppermute(given, "core", swap).astype(F32)).astype(BF16)
    parts = lax.all_to_all(pair.reshape(chips, -1, width), "chip", 0, 0, tiled=True)
    mine = jnp.sum(parts.astype(F32), axis=0, keepdims=True).astype(BF16)
    half = lax.all_to_all(jnp.broadcast_to(mine, parts.shape), "chip", 0, 0, tiled=True)
    half = half.reshape(kept.shape)
    other = lax.ppermute(half, "core", swap)
    return jnp.concatenate([jnp.where(core == 0, half, other), jnp.where(core == 0, other, half)])


def shards(embeddings, operators, plan, relations):
    e, table, history = embeddings, operators, []
    left = prepare(relations, e)
    for r in range(ROUNDS):
        right = fetch(left, plan[r])
        out = run_round(r, relations, e, left, right, table, history)
        if r == ROUNDS - 1:
            e, kept, given = out
            break
        history.append((left, out[2]))
        e, left = out[:2]
        if r == 0:
            table = out[3]
    return (e, operators - operator_rate * reduce_operators(kept, given).astype(F32))


def solution(mesh):
    pairs = jax.sharding.Mesh(mesh.devices.reshape(-1, 2), AXES)
    return jax.shard_map(
        shards,
        mesh=pairs,
        in_specs=(P(AXES, None), P(), P(), P(None, AXES)),
        out_specs=(P(AXES, None), P()),
        check_vma=False,
    )
```

```python
import functools
import math

import jax
import jax.numpy as jnp
from jax import lax
from jax.experimental import pallas as pl
from jax.experimental.pallas import tpu as pltpu
from jax.sharding import PartitionSpec as P

ROUNDS = 4
AXES = ("chip", "core")
ID_ROWS = 16
CHUNK = 256
SMALL = 128
F32 = jnp.float32
BF16 = jnp.bfloat16

embed_rate = 1.0
operator_rate = 0.02


def dot_nt(a, b):
    return lax.dot_general(a, b, (((1,), (1,)), ((), ())), preferred_element_type=F32)


def dot_nn(a, b):
    return lax.dot_general(a, b, (((1,), (0,)), ((), ())), preferred_element_type=F32)


def dot_tn(a, b):
    return lax.dot_general(a, b, (((0,), (0,)), ((), ())), preferred_element_type=F32)


def rows_at(i, size):
    return pl.ds(pl.multiple_of(i * size, size), size)


def general_gradient(k, x_ref, y_ref, s_ref, norm_ref, out_ref):
    rows, width = x_ref.shape[1:]
    scale = 1.0 / math.sqrt(width)
    in_bits = scale * math.log2(math.e)
    shift = -math.log2(scale)

    def scores(i, carry):
        col_max, col_sum = carry
        block = rows_at(i, SMALL)
        s = dot_nt(x_ref[k, block, :], y_ref[k]) * in_bits
        s_ref[block, :] = s
        row_max = jnp.max(s, axis=1, keepdims=True)
        row_sum = jnp.sum(jnp.exp2(s - row_max), axis=1, keepdims=True)
        norm_ref[block, :] = row_max + (jnp.log2(row_sum) + shift)
        new_max = jnp.maximum(col_max, jnp.max(s, axis=0, keepdims=True))
        col_sum = col_sum * jnp.exp2(col_max - new_max) + jnp.sum(
            jnp.exp2(s - new_max), axis=0, keepdims=True
        )
        return new_max, col_sum

    start = (jnp.full((1, rows), -jnp.inf, F32), jnp.zeros((1, rows), F32))
    col_max, col_sum = lax.fori_loop(0, rows // SMALL, scores, start)
    col_norm = col_max + (jnp.log2(col_sum) + shift)

    def gradient(i, carry):
        block = rows_at(i, SMALL)
        s = s_ref[block, :]
        d = jnp.exp2(s - norm_ref[block, :]) + jnp.exp2(s - col_norm)
        at = lax.broadcasted_iota(jnp.int32, d.shape, 0) + i * SMALL
        d = jnp.where(at == lax.broadcasted_iota(jnp.int32, d.shape, 1), d - 2.0 * scale, d)
        out_ref[k, block, :] = dot_nn(d.astype(BF16), y_ref[k]).astype(BF16)
        return carry

    lax.fori_loop(0, rows // SMALL, gradient, 0)


def two_way_gradient(k, x_ref, y_ref, s_ref, norm_ref, out_ref):
    rows, width = x_ref.shape[1:]
    chunks = rows // CHUNK
    scale = 1.0 / math.sqrt(width)
    in_bits = scale * math.log2(math.e)
    row_parts = []
    col_sum = jnp.zeros((1, rows), F32)
    low = high = None
    for i in range(chunks):
        block = pl.ds(i * CHUNK, CHUNK)
        e = jnp.exp2(dot_nt(x_ref[k, block, :], y_ref[k]) * in_bits)
        s_ref[block, :] = e
        row_sum = jnp.sum(e, axis=1, keepdims=True)
        col_sum = col_sum + jnp.sum(e, axis=0, keepdims=True)
        row_parts.append(scale / row_sum)
        low = row_sum if i == 0 else jnp.minimum(low, row_sum)
        high = row_sum if i == 0 else jnp.maximum(high, row_sum)
    col_part = scale / col_sum
    least = jnp.minimum(jnp.min(low), jnp.min(col_sum))
    most = jnp.maximum(jnp.max(high), jnp.max(col_sum))
    inside = jnp.logical_and(least > 2.0**-80, most < 2.0**100)

    @pl.when(inside)
    def _():
        square = (CHUNK, CHUNK)
        same = lax.broadcasted_iota(jnp.int32, square, 0) == lax.broadcasted_iota(jnp.int32, square, 1)
        diagonal = jnp.where(same, 2.0 * scale, 0.0)
        for i in range(chunks):
            block = pl.ds(i * CHUNK, CHUNK)
            strips = []
            for j in range(chunks):
                span = slice(j * CHUNK, (j + 1) * CHUNK)
                d = s_ref[block, span] * (row_parts[i] + col_part[:, span])
                strips.append((d - diagonal if i == j else d).astype(BF16))
            d = jnp.concatenate(strips, axis=1)
            out_ref[k, block, :] = dot_nn(d, y_ref[k]).astype(BF16)

    @pl.when(jnp.logical_not(inside))
    def _():
        general_gradient(k, x_ref, y_ref, s_ref, norm_ref, out_ref)


def write_payload(out_ref, value, block):
    out_ref[block, :] = value.astype(BF16)


def write_ids(out_ref, rel_ref, index):
    rows = out_ref.shape[0] - ID_ROWS
    lane = lax.broadcasted_iota(jnp.int32, (ID_ROWS, out_ref.shape[1]), 1)
    ids = jnp.zeros(lane.shape, jnp.int32)
    for b in range(rel_ref.shape[1]):
        ids = jnp.where(lane == b, rel_ref[index, b], ids)
    out_ref[pl.ds(rows, ID_ROWS), :] = ids.astype(F32).astype(BF16)


def read_ids(ids_in_ref, ids_ref):
    ids = ids_in_ref[...].astype(F32)
    lane = lax.broadcasted_iota(jnp.int32, ids.shape, 1)
    for b in range(ids_ref.shape[0]):
        ids_ref[b] = jnp.max(jnp.where(lane == b, ids, 0.0)).astype(jnp.int32)


def round_kernel(index, *refs):
    first, last = index == 0, index == ROUNDS - 1
    refs = list(refs)
    rel_ref, e_ref, l_ref, r_ref, table_ref = refs[:5]
    refs = refs[5:]
    old = [refs.pop(0) for _ in range(2 * index if last else 0)]
    core_ref = refs.pop(0) if last else None
    e_out_ref = refs.pop(0)
    outputs, refs = refs[:2], refs[2:]
    if last:
        kept_out_ref, given_out_ref = outputs
    else:
        l_out_ref, dq_ref = outputs
    ops_ref = refs.pop(0) if first else table_ref
    x_ref, y_ref, out_ref, s_ref, norm_ref, ids_ref, ids_in_ref, moved_ref, send_ref, sems = refs[:10]
    rows = moved_ref.shape[0]
    blocks = rel_ref.shape[1]
    size = rows // blocks
    every = pl.ds(0, rows)
    copies = []

    def copy(source, target):
        copies.append(pltpu.make_async_copy(source, target, sems.at[len(copies)]))
        copies[-1].start()
        return copies[-1]

    arrive = [
        copy(r_ref.at[pl.ds(rows, ID_ROWS)], ids_in_ref),
        copy(l_ref.at[every], x_ref.at[1]),
        copy(r_ref.at[every], y_ref.at[0]),
    ]
    embed_copy = copy(e_ref, moved_ref)
    if last:
        g_ref, kept_ref = refs[10:]
        arrive_old = [
            copy(old[k].at[every], kept_ref.at[k]) for k in range(2 * index)
        ]
    if first:
        for c in range(table_ref.shape[0]):
            ops_ref[c] = table_ref[c].astype(BF16)
    for one in arrive:
        one.wait()
    read_ids(ids_in_ref, ids_ref)
    for b in range(blocks):
        block = pl.ds(b * size, size)
        x_ref[0, block, :] = dot_nn(x_ref[1, block, :], ops_ref[rel_ref[index, b]]).astype(BF16)
        y_ref[1, block, :] = dot_nn(y_ref[0, block, :], ops_ref[ids_ref[b]]).astype(BF16)
    leave = []
    two_way_gradient(0, x_ref, y_ref, s_ref, norm_ref, out_ref)
    if not last:
        leave.append(copy(out_ref.at[0], dq_ref))
    two_way_gradient(1, x_ref, y_ref, s_ref, norm_ref, out_ref)
    embed_copy.wait()
    half = rows // 2
    for b in range(blocks):
        block = pl.ds(b * size, size)
        own = dot_nt(out_ref[0, block, :], ops_ref[rel_ref[index, b]])
        moved = moved_ref[block, :] - embed_rate * (own + out_ref[1, block, :].astype(F32))
        moved_ref[block, :] = moved
        if not last:
            send_ref[block, :] = moved.astype(BF16)
        if (b + 1) * size % half == 0:
            part = pl.ds((b + 1) * size - half, half)
            if not last:
                leave.append(copy(send_ref.at[part], l_out_ref.at[part]))
            leave.append(copy(moved_ref.at[part], e_out_ref.at[part]))
    if last:
        for one in arrive_old:
            one.wait()
        g_ref[...] = jnp.zeros(g_ref.shape, F32)
        for k in range(ROUNDS):
            for b in range(blocks):
                block = pl.ds(b * size, size)
                left = x_ref[1, block, :] if k == index else kept_ref[2 * k, block, :]
                grad = out_ref[0, block, :] if k == index else kept_ref[2 * k + 1, block, :]
                g_ref[rel_ref[k, b]] += dot_tn(left, grad)
        half = g_ref.shape[0] // 2
        for c in range(half):
            kept_out_ref[c] = g_ref[core_ref[0] * half + c].astype(BF16)
            given_out_ref[c] = g_ref[half - core_ref[0] * half + c].astype(BF16)
    else:
        write_ids(send_ref, rel_ref, index + 1)
        tail = pl.ds(rows, ID_ROWS)
        leave.append(copy(send_ref.at[tail], l_out_ref.at[tail]))
    for one in leave:
        one.wait()


def run_round(index, relations, e, left, right, table, history):
    first, last = index == 0, index == ROUNDS - 1
    rows, width = e.shape
    vmem = pl.BlockSpec(memory_space=pltpu.VMEM)
    hbm = pl.BlockSpec(memory_space=pltpu.HBM)
    args = [relations, e, left, right, table]
    specs = [pl.BlockSpec(memory_space=pltpu.SMEM)] + [hbm] * 3 + [vmem]
    shapes = [jax.ShapeDtypeStruct(e.shape, F32)]
    outs = [hbm]
    scratch = [pltpu.VMEM((2, rows, width), BF16)] * 3 + [
        pltpu.VMEM((rows, rows), F32),
        pltpu.VMEM((rows, 1), F32),
        pltpu.SMEM((relations.shape[1],), jnp.int32),
        pltpu.VMEM((ID_ROWS, width), BF16),
        pltpu.VMEM((rows, width), F32),
        pltpu.VMEM((rows + ID_ROWS, width), BF16),
        pltpu.SemaphoreType.DMA((16,)),
    ]
    if last:
        for old in history:
            args += old
            specs += [hbm] * 2
        args.append(lax.axis_index("core").astype(jnp.int32).reshape(1))
        specs.append(pl.BlockSpec(memory_space=pltpu.SMEM))
        half = (table.shape[0] // 2,) + table.shape[1:]
        shapes += [jax.ShapeDtypeStruct(half, BF16)] * 2
        outs += [vmem] * 2
        scratch += [pltpu.VMEM(table.shape, F32), pltpu.VMEM((2 * index, rows, width), BF16)]
    else:
        shapes += [jax.ShapeDtypeStruct(left.shape, BF16), jax.ShapeDtypeStruct(e.shape, BF16)]
        outs += [hbm] * 2
    if first:
        shapes.append(jax.ShapeDtypeStruct(table.shape, BF16))
        outs.append(vmem)
    return pl.pallas_call(
        functools.partial(round_kernel, index),
        out_shape=tuple(shapes),
        in_specs=specs,
        out_specs=tuple(outs),
        scratch_shapes=scratch,
        compiler_params=pltpu.CompilerParams(vmem_limit_bytes=60 * 2**20),
    )(*args)


def prepare(ids, e):
    line = jnp.pad(ids.astype(F32), (0, e.shape[1] - ids.shape[0]))
    tail = jnp.broadcast_to(line, (ID_ROWS, e.shape[1]))
    return jnp.concatenate([e, tail]).astype(BF16)


def keep(values):
    def kernel(in_ref, out_ref):
        out_ref[...] = in_ref[...]

    spec = pl.BlockSpec(memory_space=pltpu.VMEM)
    shape = jax.ShapeDtypeStruct(values.shape, values.dtype)
    return pl.pallas_call(kernel, out_shape=shape, in_specs=[spec], out_specs=spec)(values)


def crossing(values, mask, places, whole=None):
    count = lax.axis_size(AXES)

    def send(known):
        if known == 0:
            return keep
        route = [(i, i ^ known) for i in range(count)]
        return lambda x: lax.ppermute(x, AXES, route)

    def pick(known, left):
        if not left:
            if whole is not None and known == sum(1 << p for p in places):
                return lambda x: lax.cond(mask == whole, send(whole), send(known), x)
            return send(known)
        half = 1 << left[0]
        high, low = pick(known | half, left[1:]), pick(known, left[1:])
        return lambda x: lax.cond((mask & half) != 0, high, low, x)

    return pick(0, places)(values)


def fetch(values, mask):
    bits = lax.axis_size(AXES).bit_length() - 1
    full = (1 << bits) - 1
    values = crossing(values, mask, list(range(1, bits - 2))[::-1], full)
    rest = jnp.where(mask == full, 0, mask)
    values = crossing(values, rest, [bits - 1, bits - 2])
    return crossing(values, rest, [0])


def reduce_operators(kept, given):
    width = kept.shape[2]
    chips = lax.axis_size("chip")
    core = lax.axis_index("core")
    swap = [(0, 1), (1, 0)]
    pair = (kept.astype(F32) + lax.ppermute(given, "core", swap).astype(F32)).astype(BF16)
    parts = lax.all_to_all(pair.reshape(chips, -1, width), "chip", 0, 0, tiled=True)
    mine = jnp.sum(parts.astype(F32), axis=0, keepdims=True).astype(BF16)
    half = lax.all_to_all(jnp.broadcast_to(mine, parts.shape), "chip", 0, 0, tiled=True)
    half = half.reshape(kept.shape)
    other = lax.ppermute(half, "core", swap)
    return jnp.concatenate([jnp.where(core == 0, half, other), jnp.where(core == 0, other, half)])


def shards(embeddings, operators, plan, relations):
    e, table, history = embeddings, operators, []
    left = prepare(relations[0], e)
    for r in range(ROUNDS):
        right = fetch(left, plan[r])
        out = run_round(r, relations, e, left, right, table, history)
        if r == ROUNDS - 1:
            e, kept, given = out
            break
        history.append((left, out[2]))
        e, left = out[:2]
        if r == 0:
            table = out[3]
    return (e, operators - operator_rate * reduce_operators(kept, given).astype(F32))


def solution(mesh):
    pairs = jax.sharding.Mesh(mesh.devices.reshape(-1, 2), AXES)
    return jax.shard_map(
        shards,
        mesh=pairs,
        in_specs=(P(AXES, None), P(), P(), P(None, AXES)),
        out_specs=(P(AXES, None), P()),
        check_vma=False,
    )
```

```python
import functools
import math

import jax
import jax.numpy as jnp
from jax import lax
from jax.experimental import pallas as pl
from jax.experimental.pallas import tpu as pltpu
from jax.sharding import PartitionSpec as P

ROUNDS = 4
AXES = ("chip", "core")
ID_ROWS = 16
CHUNK = 256
SMALL = 128
F32 = jnp.float32
BF16 = jnp.bfloat16

embed_rate = 1.0
operator_rate = 0.02


def dot_nt(a, b):
    return lax.dot_general(a, b, (((1,), (1,)), ((), ())), preferred_element_type=F32)


def dot_nn(a, b):
    return lax.dot_general(a, b, (((1,), (0,)), ((), ())), preferred_element_type=F32)


def dot_tn(a, b):
    return lax.dot_general(a, b, (((0,), (0,)), ((), ())), preferred_element_type=F32)


def rows_at(i, size):
    return pl.ds(pl.multiple_of(i * size, size), size)


def general_gradient(k, x_ref, y_ref, s_ref, norm_ref, out_ref):
    rows, width = x_ref.shape[1:]
    scale = 1.0 / math.sqrt(width)
    in_bits = scale * math.log2(math.e)
    shift = -math.log2(scale)

    def scores(i, carry):
        col_max, col_sum = carry
        block = rows_at(i, SMALL)
        s = dot_nt(x_ref[k, block, :], y_ref[k]) * in_bits
        s_ref[block, :] = s
        row_max = jnp.max(s, axis=1, keepdims=True)
        row_sum = jnp.sum(jnp.exp2(s - row_max), axis=1, keepdims=True)
        norm_ref[block, :] = row_max + (jnp.log2(row_sum) + shift)
        new_max = jnp.maximum(col_max, jnp.max(s, axis=0, keepdims=True))
        col_sum = col_sum * jnp.exp2(col_max - new_max) + jnp.sum(
            jnp.exp2(s - new_max), axis=0, keepdims=True
        )
        return new_max, col_sum

    start = (jnp.full((1, rows), -jnp.inf, F32), jnp.zeros((1, rows), F32))
    col_max, col_sum = lax.fori_loop(0, rows // SMALL, scores, start)
    col_norm = col_max + (jnp.log2(col_sum) + shift)

    def gradient(i, carry):
        block = rows_at(i, SMALL)
        s = s_ref[block, :]
        d = jnp.exp2(s - norm_ref[block, :]) + jnp.exp2(s - col_norm)
        at = lax.broadcasted_iota(jnp.int32, d.shape, 0) + i * SMALL
        d = jnp.where(at == lax.broadcasted_iota(jnp.int32, d.shape, 1), d - 2.0 * scale, d)
        out_ref[k, block, :] = dot_nn(d.astype(BF16), y_ref[k]).astype(BF16)
        return carry

    lax.fori_loop(0, rows // SMALL, gradient, 0)


def two_way_gradient(k, x_ref, y_ref, s_ref, norm_ref, out_ref):
    rows, width = x_ref.shape[1:]
    chunks = rows // CHUNK
    scale = 1.0 / math.sqrt(width)
    in_bits = scale * math.log2(math.e)
    row_parts = []
    col_sum = jnp.zeros((1, rows), F32)
    low = high = None
    for i in range(chunks):
        block = pl.ds(i * CHUNK, CHUNK)
        e = jnp.exp2(dot_nt(x_ref[k, block, :], y_ref[k]) * in_bits)
        s_ref[block, :] = e
        row_sum = jnp.sum(e, axis=1, keepdims=True)
        col_sum = col_sum + jnp.sum(e, axis=0, keepdims=True)
        row_parts.append(scale / row_sum)
        low = row_sum if i == 0 else jnp.minimum(low, row_sum)
        high = row_sum if i == 0 else jnp.maximum(high, row_sum)
    col_part = scale / col_sum
    least = jnp.minimum(jnp.min(low), jnp.min(col_sum))
    most = jnp.maximum(jnp.max(high), jnp.max(col_sum))
    inside = jnp.logical_and(least > 2.0**-80, most < 2.0**100)

    @pl.when(inside)
    def _():
        square = (CHUNK, CHUNK)
        same = lax.broadcasted_iota(jnp.int32, square, 0) == lax.broadcasted_iota(jnp.int32, square, 1)
        diagonal = jnp.where(same, 2.0 * scale, 0.0)
        for i in range(chunks):
            block = pl.ds(i * CHUNK, CHUNK)
            strips = []
            for j in range(chunks):
                span = slice(j * CHUNK, (j + 1) * CHUNK)
                d = s_ref[block, span] * (row_parts[i] + col_part[:, span])
                strips.append((d - diagonal if i == j else d).astype(BF16))
            d = jnp.concatenate(strips, axis=1)
            out_ref[k, block, :] = dot_nn(d, y_ref[k]).astype(BF16)

    @pl.when(jnp.logical_not(inside))
    def _():
        general_gradient(k, x_ref, y_ref, s_ref, norm_ref, out_ref)


def write_payload(out_ref, value, block):
    out_ref[block, :] = value.astype(BF16)


def write_ids(out_ref, rel_ref, index):
    rows = out_ref.shape[0] - ID_ROWS
    lane = lax.broadcasted_iota(jnp.int32, (ID_ROWS, out_ref.shape[1]), 1)
    ids = jnp.zeros(lane.shape, jnp.int32)
    for b in range(rel_ref.shape[1]):
        ids = jnp.where(lane == b, rel_ref[index, b], ids)
    out_ref[pl.ds(rows, ID_ROWS), :] = ids.astype(F32).astype(BF16)


def read_ids(ids_in_ref, ids_ref):
    ids = ids_in_ref[...].astype(F32)
    lane = lax.broadcasted_iota(jnp.int32, ids.shape, 1)
    for b in range(ids_ref.shape[0]):
        ids_ref[b] = jnp.max(jnp.where(lane == b, ids, 0.0)).astype(jnp.int32)


def prepare_kernel(rel_ref, e_ref, out_ref):
    write_payload(out_ref, e_ref[...], pl.ds(0, e_ref.shape[0]))
    write_ids(out_ref, rel_ref, 0)


def round_kernel(index, *refs):
    first, last = index == 0, index == ROUNDS - 1
    refs = list(refs)
    rel_ref, e_ref, l_ref, r_ref, table_ref = refs[:5]
    refs = refs[5:]
    old = [refs.pop(0) for _ in range(2 * index if last else 0)]
    core_ref = refs.pop(0) if last else None
    e_out_ref = refs.pop(0)
    outputs, refs = refs[:2], refs[2:]
    if last:
        kept_out_ref, given_out_ref = outputs
    else:
        l_out_ref, dq_ref = outputs
    ops_ref = refs.pop(0) if first else table_ref
    x_ref, y_ref, out_ref, s_ref, norm_ref, ids_ref, ids_in_ref, moved_ref, send_ref, sems = refs[:10]
    rows = moved_ref.shape[0]
    blocks = rel_ref.shape[1]
    size = rows // blocks
    every = pl.ds(0, rows)
    copies = []

    def copy(source, target):
        copies.append(pltpu.make_async_copy(source, target, sems.at[len(copies)]))
        copies[-1].start()
        return copies[-1]

    arrive = [
        copy(r_ref.at[pl.ds(rows, ID_ROWS)], ids_in_ref),
        copy(l_ref.at[every], x_ref.at[1]),
        copy(r_ref.at[every], y_ref.at[0]),
    ]
    embed_copy = copy(e_ref, moved_ref)
    if last:
        g_ref, kept_ref = refs[10:]
        arrive_old = [
            copy(old[k].at[every], kept_ref.at[k]) for k in range(2 * index)
        ]
    if first:
        for c in range(table_ref.shape[0]):
            ops_ref[c] = table_ref[c].astype(BF16)
    for one in arrive:
        one.wait()
    read_ids(ids_in_ref, ids_ref)
    for b in range(blocks):
        block = pl.ds(b * size, size)
        x_ref[0, block, :] = dot_nn(x_ref[1, block, :], ops_ref[rel_ref[index, b]]).astype(BF16)
        y_ref[1, block, :] = dot_nn(y_ref[0, block, :], ops_ref[ids_ref[b]]).astype(BF16)
    leave = []
    two_way_gradient(0, x_ref, y_ref, s_ref, norm_ref, out_ref)
    if not last:
        leave.append(copy(out_ref.at[0], dq_ref))
    two_way_gradient(1, x_ref, y_ref, s_ref, norm_ref, out_ref)
    embed_copy.wait()
    half = rows // 2
    for b in range(blocks):
        block = pl.ds(b * size, size)
        own = dot_nt(out_ref[0, block, :], ops_ref[rel_ref[index, b]])
        moved = moved_ref[block, :] - embed_rate * (own + out_ref[1, block, :].astype(F32))
        moved_ref[block, :] = moved
        if not last:
            send_ref[block, :] = moved.astype(BF16)
        if (b + 1) * size % half == 0:
            part = pl.ds((b + 1) * size - half, half)
            if not last:
                leave.append(copy(send_ref.at[part], l_out_ref.at[part]))
            leave.append(copy(moved_ref.at[part], e_out_ref.at[part]))
    if last:
        for one in arrive_old:
            one.wait()
        g_ref[...] = jnp.zeros(g_ref.shape, F32)
        for k in range(ROUNDS):
            for b in range(blocks):
                block = pl.ds(b * size, size)
                left = x_ref[1, block, :] if k == index else kept_ref[2 * k, block, :]
                grad = out_ref[0, block, :] if k == index else kept_ref[2 * k + 1, block, :]
                g_ref[rel_ref[k, b]] += dot_tn(left, grad)
        half = g_ref.shape[0] // 2
        for c in range(half):
            kept_out_ref[c] = g_ref[core_ref[0] * half + c].astype(BF16)
            given_out_ref[c] = g_ref[half - core_ref[0] * half + c].astype(BF16)
    else:
        write_ids(send_ref, rel_ref, index + 1)
        tail = pl.ds(rows, ID_ROWS)
        leave.append(copy(send_ref.at[tail], l_out_ref.at[tail]))
    for one in leave:
        one.wait()


def run_round(index, relations, e, left, right, table, history):
    first, last = index == 0, index == ROUNDS - 1
    rows, width = e.shape
    vmem = pl.BlockSpec(memory_space=pltpu.VMEM)
    hbm = pl.BlockSpec(memory_space=pltpu.HBM)
    args = [relations, e, left, right, table]
    specs = [pl.BlockSpec(memory_space=pltpu.SMEM)] + [hbm] * 3 + [vmem]
    shapes = [jax.ShapeDtypeStruct(e.shape, F32)]
    outs = [hbm]
    scratch = [pltpu.VMEM((2, rows, width), BF16)] * 3 + [
        pltpu.VMEM((rows, rows), F32),
        pltpu.VMEM((rows, 1), F32),
        pltpu.SMEM((relations.shape[1],), jnp.int32),
        pltpu.VMEM((ID_ROWS, width), BF16),
        pltpu.VMEM((rows, width), F32),
        pltpu.VMEM((rows + ID_ROWS, width), BF16),
        pltpu.SemaphoreType.DMA((16,)),
    ]
    if last:
        for old in history:
            args += old
            specs += [hbm] * 2
        args.append(lax.axis_index("core").astype(jnp.int32).reshape(1))
        specs.append(pl.BlockSpec(memory_space=pltpu.SMEM))
        half = (table.shape[0] // 2,) + table.shape[1:]
        shapes += [jax.ShapeDtypeStruct(half, BF16)] * 2
        outs += [vmem] * 2
        scratch += [pltpu.VMEM(table.shape, F32), pltpu.VMEM((2 * index, rows, width), BF16)]
    else:
        shapes += [jax.ShapeDtypeStruct(left.shape, BF16), jax.ShapeDtypeStruct(e.shape, BF16)]
        outs += [hbm] * 2
    if first:
        shapes.append(jax.ShapeDtypeStruct(table.shape, BF16))
        outs.append(vmem)
    return pl.pallas_call(
        functools.partial(round_kernel, index),
        out_shape=tuple(shapes),
        in_specs=specs,
        out_specs=tuple(outs),
        scratch_shapes=scratch,
        compiler_params=pltpu.CompilerParams(vmem_limit_bytes=60 * 2**20),
    )(*args)


def prepare(rel, e):
    rows, width = e.shape
    return pl.pallas_call(
        prepare_kernel,
        out_shape=jax.ShapeDtypeStruct((rows + ID_ROWS, width), BF16),
        in_specs=[pl.BlockSpec(memory_space=pltpu.SMEM), pl.BlockSpec(memory_space=pltpu.VMEM)],
        out_specs=pl.BlockSpec(memory_space=pltpu.VMEM),
    )(rel, e)


def keep(values):
    def kernel(in_ref, out_ref):
        out_ref[...] = in_ref[...]

    spec = pl.BlockSpec(memory_space=pltpu.VMEM)
    shape = jax.ShapeDtypeStruct(values.shape, values.dtype)
    return pl.pallas_call(kernel, out_shape=shape, in_specs=[spec], out_specs=spec)(values)


def send(known):
    if known == 0:
        return keep
    route = [(i, i ^ known) for i in range(lax.axis_size(AXES))]
    return lambda x: lax.ppermute(x, AXES, route)


def crossing(values, mask, places):
    def pick(known, left):
        if not left:
            return send(known)
        half = 1 << left[0]
        high, low = pick(known | half, left[1:]), pick(known, left[1:])
        return lambda x: lax.cond((mask & half) != 0, high, low, x)

    return pick(0, places)(values)


def fetch(values, mask):
    bits = lax.axis_size(AXES).bit_length() - 1
    full = (1 << bits) - 1

    def staged(x):
        x = crossing(x, mask, list(range(1, bits - 2))[::-1])
        x = crossing(x, mask, [bits - 1, bits - 2])
        return crossing(x, mask, [0])

    return lax.cond(mask == full, send(full), staged, values)


def reduce_operators(kept, given):
    width = kept.shape[2]
    chips = lax.axis_size("chip")
    core = lax.axis_index("core")
    swap = [(0, 1), (1, 0)]
    pair = (kept.astype(F32) + lax.ppermute(given, "core", swap).astype(F32)).astype(BF16)
    parts = lax.all_to_all(pair.reshape(chips, -1, width), "chip", 0, 0, tiled=True)
    mine = jnp.sum(parts.astype(F32), axis=0, keepdims=True).astype(BF16)
    half = lax.all_to_all(jnp.broadcast_to(mine, parts.shape), "chip", 0, 0, tiled=True)
    half = half.reshape(kept.shape)
    other = lax.ppermute(half, "core", swap)
    return jnp.concatenate([jnp.where(core == 0, half, other), jnp.where(core == 0, other, half)])


def shards(embeddings, operators, plan, relations):
    e, table, history = embeddings, operators, []
    left = prepare(relations, e)
    for r in range(ROUNDS):
        right = fetch(left, plan[r])
        out = run_round(r, relations, e, left, right, table, history)
        if r == ROUNDS - 1:
            e, kept, given = out
            break
        history.append((left, out[2]))
        e, left = out[:2]
        if r == 0:
            table = out[3]
    return (e, operators - operator_rate * reduce_operators(kept, given).astype(F32))


def solution(mesh):
    pairs = jax.sharding.Mesh(mesh.devices.reshape(-1, 2), AXES)
    return jax.shard_map(
        shards,
        mesh=pairs,
        in_specs=(P(AXES, None), P(), P(), P(None, AXES)),
        out_specs=(P(AXES, None), P()),
        check_vma=False,
    )
```
